512 devices in a mesh: row: 64 (over y, x, z_hi, core), col: 8 (over z_lo).
Axes of the slice: x: 4, y: 4, z: 16 (z_hi: 2, z_lo: 8; z = z_hi * 8 + z_lo), core: 2. Of those that a mesh axis runs over, the one named last changes fastest.
Arguments:
- flow_state: float32 [4, 128, 256, 1024], P(None, 'row', 'col'), may hold values from -6 to 6
- spacing: float32 [128], replicated, may hold values from 0.004 to 0.012
- diffusivity: float32 [4], replicated, may hold values from 0.03 to 0.1
Outputs:
- flow_next: float32 [4, 128, 256, 1024], P(None, 'row', 'col')
The draws below stay inside these ranges and needn't reach their ends.
All inputs are finite; a program needn't handle non-finite values.
Results may differ from the reference program's by a relative error of at most 0.00023.
Values sent between devices are 32-bit elements; how exact they have to be, the bound alone decides.
No kernel may reach another device: no remote copies, remote signals or barrier semaphores. Data moves between devices by JAX's collectives and lax.ppermute only.
A program may use at most 64 MiB of HBM per device.

```python
import math
import jax
import jax.numpy as jnp
from jax import lax

NZ = 128
NX = 1024
NY = 256


def steps_of(own_key, shape, shards, least, largest):
    factor_of, own = 1.0, jax.random.fold_in(own_key, 6)
    for position, parts in shards:
        draws = jnp.exp(jax.random.uniform(jax.random.fold_in(own, position), (parts,), jnp.float32, least / len(shards), largest / len(shards)))
        factor_of = factor_of * jnp.repeat(draws, shape[position] // parts).reshape([-1 if axis == position else 1 for axis in range(len(shape))])
    return factor_of


def noise(key, extent, spread, limit, shards=(), kind=jnp.bfloat16):
    values = spread * jax.random.normal(key, extent, jnp.float32)
    if shards:
        values = values * steps_of(key, extent, shards, -0.22, 0.18)
    return jnp.clip(values, -limit, limit).astype(kind)


def setup_inputs(seed: int = 0) -> dict:
    key_of = jax.random.split(jax.random.key(seed), 4)
    flow_state = noise(key_of[0], (4, NZ, NY, NX), 1.0, 6.0, ((1, 64), (2, 8)), jnp.float32)
    spacing = jnp.clip(jnp.exp(jax.random.uniform(key_of[1], (NZ,), jnp.float32, math.log(0.004), math.log(0.012))), 0.004, 0.012)
    diffusivity = jnp.clip(jnp.exp(jax.random.uniform(key_of[2], (4,), jnp.float32, math.log(0.03), math.log(0.1))), 0.03, 0.1)
    return {"flow_state": flow_state, "spacing": spacing, "diffusivity": diffusivity}


time_step = 0.02
cell_width = 0.1
buoyancy = 1.0

def wall_geometry(spacing):
    centres = jnp.cumsum(spacing)
    positions = jnp.concatenate([centres[:1] - spacing[:1], centres, centres[-1:] + spacing[-1:]])
    gap_below = positions[1:-1] - positions[:-2]
    gap_above = positions[2:] - positions[1:-1]
    across = positions[2:] - positions[:-2]
    return (gap_below, gap_above, across)

def line_system(spacing, diffusivity):
    gap_below, gap_above, across = wall_geometry(spacing)
    diffuse_rate = time_step * diffusivity[:, None]
    lower_band = -2.0 * diffuse_rate / (across * gap_below)
    upper_band = -2.0 * diffuse_rate / (across * gap_above)
    middle = 1.0 - lower_band - upper_band
    levels = jnp.arange(spacing.shape[0])
    lower_band = jnp.where(levels == 0, 0.0, lower_band)
    upper_band = jnp.where(levels == spacing.shape[0] - 1, 0.0, upper_band)
    return (lower_band, middle, upper_band)

def advance(centre, speeds, z_down, z_up, y_left, y_right, across, diffusivity, forcing):
    x_left = jnp.roll(centre, 1, axis=-1)
    x_right = jnp.roll(centre, -1, axis=-1)
    advection = speeds[0] * (x_right - x_left) / (2.0 * cell_width)
    advection = advection + speeds[1] * (y_right - y_left) / (2.0 * cell_width)
    advection = advection + speeds[2] * (z_up - z_down) / across[:, None, None]
    laplace = (x_right + x_left - 2.0 * centre) / cell_width ** 2
    laplace = laplace + (y_right + y_left - 2.0 * centre) / cell_width ** 2
    return centre + time_step * (diffusivity * laplace - advection + forcing)

def reference(flow_state, spacing, diffusivity):
    gap_below, gap_above, across = wall_geometry(spacing)
    lower_band, middle, upper_band = line_system(spacing, diffusivity)
    results = []
    for component in range(4):
        centre = flow_state[component]
        z_padded = jnp.pad(centre, ((1, 1), (0, 0), (0, 0)))
        if component == 2:
            forcing = buoyancy * flow_state[3]
        elif component == 3:
            forcing = flow_state[2]
        else:
            forcing = 0.0
        stepped = advance(centre, flow_state, z_padded[:-2], z_padded[2:], jnp.roll(centre, 1, axis=1), jnp.roll(centre, -1, axis=1), across, diffusivity[component], forcing)
        solved = lax.linalg.tridiagonal_solve(lower_band[component], middle[component], upper_band[component], stepped.reshape(stepped.shape[0], -1))
        results.append(solved.reshape(centre.shape))
    return jnp.stack(results)
```

```python
import jax
import jax.numpy as jnp
import numpy as np
from jax import lax
from jax.experimental import pallas as pl
from jax.experimental.pallas import tpu as pltpu
from jax.sharding import Mesh
from jax.sharding import PartitionSpec as P

time_step = 0.02
cell_width = 0.1
buoyancy = 1.0

AXES = ("y", "x", "zh", "core", "zl")
ROW = AXES[:4]
PLANE = AXES[:3]
LIMIT = 48 * 2**20


def whole(space=pltpu.VMEM):
    return pl.BlockSpec(memory_space=space)


def params():
    return pltpu.CompilerParams(vmem_limit_bytes=LIMIT)


def prefix(matrix, lane, backward):
    a, b, c, d = matrix
    step = 1
    while step < 128:
        by = 128 - step if backward else step
        edge = lane >= 128 - step if backward else lane < step
        pa, pb, pc, pd = (pltpu.roll(m, by, 1) for m in (a, b, c, d))
        pa, pb = jnp.where(edge, 1.0, pa), jnp.where(edge, 0.0, pb)
        pc, pd = jnp.where(edge, 0.0, pc), jnp.where(edge, 1.0, pd)
        a, b, c, d = a * pa + b * pc, a * pb + b * pd, c * pa + d * pc, c * pb + d * pd
        scale = 1.0 / (a + b + c + d)
        a, b, c, d = a * scale, b * scale, c * scale, d * scale
        step *= 2
    return (a + b) / (c + d)


def chip_index():
    return (lax.axis_index("y") * 4 + lax.axis_index("x")) * 2 + lax.axis_index("zh")


def coefficients_kernel(spacing_ref, diffusivity_ref, own_ref, scan_ref):
    shape = (8, 128)
    lane = lax.broadcasted_iota(jnp.int32, shape, 1)
    row = lax.broadcasted_iota(jnp.int32, shape, 0)
    below = jnp.broadcast_to(spacing_ref[...], shape)
    above = jnp.where(lane == 127, below, pltpu.roll(below, 127, 1))
    across = below + above
    rate = jnp.full(shape, diffusivity_ref[3], jnp.float32)
    for component in range(3):
        rate = jnp.where(row % 4 == component, diffusivity_ref[component], rate)
    rate = time_step * rate
    low, up = 2.0 * rate / (across * below), 2.0 * rate / (across * above)
    up_before = jnp.where(lane == 0, 0.0, pltpu.roll(up, 1, 1))
    low_after = jnp.where(lane == 127, 0.0, pltpu.roll(low, 127, 1))
    one = jnp.ones(shape, jnp.float32)
    t = prefix((1.0 + low, up_before, one, up_before), lane, False)
    tau = prefix((1.0 + up, low_after, one, low_after), lane, True)
    r = jnp.where(lane == 0, 0.0, low / (low + tau))
    s = jnp.where(lane == 127, 0.0, up / (up + t))
    g = 1.0 / (t + tau - 1.0)
    rs = jnp.where(row < 4, r, s)
    gc = jnp.where(row < 4, g, time_step / across)
    four = rs * pltpu.roll(rs, 127, 1)
    four = four * pltpu.roll(four, 126, 1)
    scan_ref[...] = four
    turn = lax.rem(129 - 4 * chip_index(), 128)
    own_ref[0:8, :] = pltpu.roll(rs, turn, 1)
    own_ref[8:16, :] = pltpu.roll(gc, turn, 1)


def local_kernel(
    own_ref, other_ref, same_ref, cross_ref, w3_ref, w4_ref, cf_ref, dif_ref, part_ref, send_ref
):
    core = lax.axis_index("core")
    first = core == 0
    sub = lax.broadcasted_iota(jnp.int32, (8, 1024), 0)
    rate = time_step / (2.0 * cell_width)

    def tile(c, level, rows):
        return jnp.where(
            core == level // 2, own_ref[c, level % 2, rows, :], other_ref[c, level % 2, rows, :]
        )

    def far(c, level):
        line = 2 * c + level % 2
        return jnp.where(
            core == level // 2, same_ref[line : line + 1, :], cross_ref[line : line + 1, :]
        )

    for half in range(2):
        rows = pl.ds(pl.multiple_of(core * 16 + 8 * half, 8), 8)
        here = slice(8 * half, 8 * half + 8)
        w_low = jnp.where(first, w3_ref[here, :], w4_ref[here, :])
        w_high = jnp.where(first, w4_ref[here, :], w3_ref[here, :])
        w_low, w_high = w_low * -cf_ref[12, 0], w_high * cf_ref[12, 5]
        u = [tile(0, level, rows) * rate for level in range(4)]
        v = [tile(1, level, rows) * rate for level in range(4)]
        w = [tile(2, level, rows) for level in range(4)]
        wc = [w[level] * cf_ref[12, level + 1] for level in range(4)]
        for c in range(4):
            r = [cf_ref[c, j] for j in range(6)]
            s = [cf_ref[4 + c, j] for j in range(6)]
            g = [cf_ref[8 + c, j] for j in range(6)]
            spread = dif_ref[c] * (time_step / cell_width**2)
            q = w if c == 2 else [tile(c, level, rows) for level in range(4)]
            gs = []
            for level in range(4):
                centre = q[level]
                left, right = pltpu.roll(centre, 1, 1), pltpu.roll(centre, 1023, 1)
                if half == 0:
                    top = jnp.where(first, far(c, level), tile(c, level, slice(15, 16)))
                    bottom = tile(c, level, pl.ds(pl.multiple_of(core * 16 + 8, 8), 8))[:1]
                else:
                    top = tile(c, level, pl.ds(pl.multiple_of(core * 16, 8), 8))[7:]
                    bottom = jnp.where(first, tile(c, level, slice(16, 17)), far(c, level))
                front = jnp.where(sub == 0, top, pltpu.roll(centre, 1, 0))
                back = jnp.where(sub == 7, bottom, pltpu.roll(centre, 7, 0))
                total = centre + spread * ((left + right) + (front + back) - 4.0 * centre)
                total = total - u[level] * (right - left) - v[level] * (back - front)
                if level == 0:
                    total = total - wc[0] * q[1]
                elif level == 3:
                    total = total + wc[3] * q[2]
                else:
                    total = total - wc[level] * (q[level + 1] - q[level - 1])
                if c == 2:
                    total = total + (time_step * buoyancy) * tile(3, level, rows)
                elif c == 3:
                    total = total + time_step * w[level]
                gs.append(g[level + 1] * total)
            g_low, g_high = g[0] * (w_low * q[0]), g[5] * (w_high * q[3])
            a = [r[1] * g_low + gs[0]]
            for level in range(1, 4):
                a.append(r[level + 1] * a[-1] + gs[level])
            p = r[5] * a[3] + g_high
            b = s[4] * g_high
            part_ref[c, 3, here, :] = a[3] + b
            for level in (2, 1, 0):
                b = s[level + 1] * (b + gs[level + 1])
                part_ref[c, level, here, :] = a[level] + b
            b = s[0] * (b + gs[0]) + g_low
            for block in range(8):
                lanes = slice(128 * block, 128 * block + 128)
                send_ref[8 * half + block, c] = p[:, lanes]
                send_ref[16 + 8 * half + block, c] = b[:, lanes]


def scan_kernel(in_ref, cf_ref, out_ref):
    upward = lax.axis_index("y") < 2

    @pl.when(upward)
    def _():
        for c in range(4):
            carry = jnp.zeros((8, 128), jnp.float32)
            for chip in range(32):
                out_ref[chip, c] = carry
                carry = cf_ref[c, 4 * chip + 1] * carry + in_ref[chip, c]

    @pl.when(jnp.logical_not(upward))
    def _():
        for c in range(4):
            carry = jnp.zeros((8, 128), jnp.float32)
            for chip in range(31, -1, -1):
                out_ref[chip, c] = carry
                carry = cf_ref[4 + c, (4 * chip + 127) % 128] * carry + in_ref[chip, c]


def finish_kernel(part_ref, carry_ref, cf_ref, out_ref, send_ref):
    core = lax.axis_index("core")
    for c in range(4):
        r = [cf_ref[c, j] for j in range(6)]
        s = [cf_ref[4 + c, j] for j in range(6)]
        up = [1.0, r[2], r[2] * r[3], r[2] * r[3] * r[4]]
        down = [s[1] * s[2] * s[3], s[2] * s[3], s[3], 1.0]
        for half in range(2):
            here = slice(8 * half, 8 * half + 8)
            rows = pl.ds(pl.multiple_of(core * 16 + 8 * half, 8), 8)
            for block in range(8):
                lanes = slice(128 * block, 128 * block + 128)
                p = carry_ref[8 * half + block, c]
                q = carry_ref[16 + 8 * half + block, c]
                x = [
                    part_ref[c, level, here, lanes] + up[level] * p + down[level] * q
                    for level in range(4)
                ]
                for k in range(2):
                    out_ref[c, k, rows, lanes] = jnp.where(core == 0, x[k], x[2 + k])
                    send_ref[c, k, here, lanes] = jnp.where(core == 0, x[2 + k], x[k])


def shards(flow_state, spacing, diffusivity):
    core = lax.axis_index("core")
    f32 = jnp.float32

    def route(value, axes, sizes, to):
        pairs = []
        for source in range(int(np.prod(sizes))):
            target = to(*(int(i) for i in np.unravel_index(source, sizes)))
            if target is not None:
                pairs.append((source, target))
        return lax.ppermute(value, axes, pairs)

    def level_rows(start):
        at = (2, core, start, 0)
        return lax.dynamic_slice(flow_state, at, (1, 1, 16, 1024)).reshape(16, 1024)

    def edge_row(start):
        return lax.dynamic_slice_in_dim(flow_state, start, 1, 2).reshape(8, 1024)

    def within(chip, k):
        return 2 * chip + k if 0 <= chip < 32 else None

    def by_chip(turned):
        def to(chip, k):
            return within(chip + 1 if k else chip - 1, 1 - k if turned else k)

        return to

    def by_col(turned):
        def to(k, z):
            return (1 - k if turned else k) * 8 + (z + (-1 if k != turned else 1)) % 8

        return to

    w3 = route(level_rows(16 * (1 - core)), ROW, (32, 2), by_chip(True))
    w4 = route(level_rows(16 * core), ROW, (32, 2), by_chip(False))
    same = route(edge_row(31 * (1 - core)), ("core", "zl"), (2, 8), by_col(False))
    cross = route(edge_row(31 * core), ("core", "zl"), (2, 8), by_col(True))
    other = lax.ppermute(flow_state, "core", [(0, 1), (1, 0)])

    own_cf, scan_cf = pl.pallas_call(
        coefficients_kernel,
        out_shape=(jax.ShapeDtypeStruct((16, 128), f32), jax.ShapeDtypeStruct((8, 128), f32)),
        in_specs=[whole(), whole(pltpu.SMEM)],
        out_specs=(whole(), whole()),
        name="coefficients",
    )(spacing.reshape(1, 128), diffusivity)

    part, moments = pl.pallas_call(
        local_kernel,
        out_shape=(
            jax.ShapeDtypeStruct((4, 4, 16, 1024), f32),
            jax.ShapeDtypeStruct((32, 4, 8, 128), f32),
        ),
        in_specs=[whole()] * 6 + [whole(pltpu.SMEM)] * 2,
        out_specs=(whole(), whole()),
        compiler_params=params(),
        name="local_step",
    )(flow_state, other, same, cross, w3, w4, own_cf, diffusivity)

    arrived = lax.all_to_all(moments, PLANE, split_axis=0, concat_axis=0, tiled=True)
    carried = pl.pallas_call(
        scan_kernel,
        out_shape=jax.ShapeDtypeStruct((32, 4, 8, 128), f32),
        in_specs=[whole(), whole(pltpu.SMEM)],
        out_specs=whole(),
        compiler_params=params(),
        name="scan_chips",
    )(arrived, scan_cf)
    returned = lax.all_to_all(carried, PLANE, split_axis=0, concat_axis=0, tiled=True)

    kept, leaving = pl.pallas_call(
        finish_kernel,
        out_shape=(
            jax.ShapeDtypeStruct((4, 2, 32, 1024), f32),
            jax.ShapeDtypeStruct((4, 2, 16, 1024), f32),
        ),
        in_specs=[whole(), whole(), whole(pltpu.SMEM)],
        out_specs=(whole(), whole()),
        compiler_params=params(),
        name="finish",
    )(part, returned, own_cf)
    back = lax.ppermute(leaving, "core", [(0, 1), (1, 0)])
    return lax.dynamic_update_slice_in_dim(kept, back, 16 * (1 - core), 2)


def solution(mesh):
    fine = Mesh(mesh.devices.reshape(4, 4, 2, 2, 8), AXES)
    field = P(None, ROW, "zl", None)
    return jax.shard_map(
        shards, mesh=fine, in_specs=(field, P(), P()), out_specs=field, check_vma=False
    )
```

```python
import jax
import jax.numpy as jnp
import numpy as np
from jax import lax
from jax.experimental import pallas as pl
from jax.experimental.pallas import tpu as pltpu
from jax.sharding import Mesh
from jax.sharding import PartitionSpec as P

time_step = 0.02
cell_width = 0.1
buoyancy = 1.0

AXES = ("y", "x", "zh", "core", "zl")
ROW = AXES[:4]
PLANE = AXES[:3]
LIMIT = 48 * 2**20


def whole(space=pltpu.VMEM):
    return pl.BlockSpec(memory_space=space)


def params():
    return pltpu.CompilerParams(vmem_limit_bytes=LIMIT)


def prefix(matrix, lane, backward):
    a, b, c, d = matrix
    step = 1
    while step < 128:
        by = 128 - step if backward else step
        edge = lane >= 128 - step if backward else lane < step
        pa, pb, pc, pd = (pltpu.roll(m, by, 1) for m in (a, b, c, d))
        pa, pb = jnp.where(edge, 1.0, pa), jnp.where(edge, 0.0, pb)
        pc, pd = jnp.where(edge, 0.0, pc), jnp.where(edge, 1.0, pd)
        a, b, c, d = a * pa + b * pc, a * pb + b * pd, c * pa + d * pc, c * pb + d * pd
        scale = 1.0 / (a + b + c + d)
        a, b, c, d = a * scale, b * scale, c * scale, d * scale
        step *= 2
    return (a + b) / (c + d)


def chip_index():
    return (lax.axis_index("y") * 4 + lax.axis_index("x")) * 2 + lax.axis_index("zh")


def coefficients_kernel(spacing_ref, diffusivity_ref, own_ref, scan_ref):
    shape = (8, 128)
    lane = lax.broadcasted_iota(jnp.int32, shape, 1)
    row = lax.broadcasted_iota(jnp.int32, shape, 0)
    below = jnp.broadcast_to(spacing_ref[...], shape)
    above = jnp.where(lane == 127, below, pltpu.roll(below, 127, 1))
    across = below + above
    rate = jnp.full(shape, diffusivity_ref[3], jnp.float32)
    for component in range(3):
        rate = jnp.where(row % 4 == component, diffusivity_ref[component], rate)
    rate = time_step * rate
    low, up = 2.0 * rate / (across * below), 2.0 * rate / (across * above)
    up_before = jnp.where(lane == 0, 0.0, pltpu.roll(up, 1, 1))
    low_after = jnp.where(lane == 127, 0.0, pltpu.roll(low, 127, 1))
    one = jnp.ones(shape, jnp.float32)
    t = prefix((1.0 + low, up_before, one, up_before), lane, False)
    tau = prefix((1.0 + up, low_after, one, low_after), lane, True)
    r = jnp.where(lane == 0, 0.0, low / (low + tau))
    s = jnp.where(lane == 127, 0.0, up / (up + t))
    g = 1.0 / (t + tau - 1.0)
    rs = jnp.where(row < 4, r, s)
    gc = jnp.where(row < 4, g, time_step / across)
    four = rs * pltpu.roll(rs, 127, 1)
    four = four * pltpu.roll(four, 126, 1)
    scan_ref[...] = four
    turn = lax.rem(129 - 4 * chip_index(), 128)
    own_ref[0:8, :] = pltpu.roll(rs, turn, 1)
    own_ref[8:16, :] = pltpu.roll(gc, turn, 1)


def ends_kernel(own_ref, other_ref, out_ref):
    first = lax.axis_index("core") == 0
    for line in range(8):
        c, k = line // 2, line % 2
        for at, ref in ((line, own_ref), (8 + line, other_ref)):
            out_ref[at : at + 1, :] = jnp.where(first, ref[c, k, 0:1, :], ref[c, k, 31:32, :])


def local_kernel(own_ref, other_ref, halo_ref, cf_ref, dif_ref, part_ref, send_ref):
    core = lax.axis_index("core")
    first = core == 0
    sub = lax.broadcasted_iota(jnp.int32, (8, 1024), 0)
    rate = time_step / (2.0 * cell_width)

    def tile(c, level, rows):
        return jnp.where(
            core == level // 2, own_ref[c, level % 2, rows, :], other_ref[c, level % 2, rows, :]
        )

    def far(c, level):
        line = 2 * c + level % 2
        return jnp.where(
            core == level // 2, halo_ref[8 + line : 9 + line, :], halo_ref[line : line + 1, :]
        )

    for half in range(2):
        rows = pl.ds(pl.multiple_of(core * 16 + 8 * half, 8), 8)
        here = slice(8 * half, 8 * half + 8)
        u = [tile(0, level, rows) * rate for level in range(4)]
        v = [tile(1, level, rows) * rate for level in range(4)]
        w = [tile(2, level, rows) for level in range(4)]
        wc = [w[level] * cf_ref[12, level + 1] for level in range(4)]
        for c in range(4):
            r = [cf_ref[c, j] for j in range(6)]
            s = [cf_ref[4 + c, j] for j in range(6)]
            g = [cf_ref[8 + c, j] for j in range(6)]
            spread = dif_ref[c] * (time_step / cell_width**2)
            q = w if c == 2 else [tile(c, level, rows) for level in range(4)]
            gs = []
            for level in range(4):
                centre = q[level]
                left, right = pltpu.roll(centre, 1, 1), pltpu.roll(centre, 1023, 1)
                if half == 0:
                    top = jnp.where(first, far(c, level), tile(c, level, slice(15, 16)))
                    bottom = tile(c, level, pl.ds(pl.multiple_of(core * 16 + 8, 8), 8))[:1]
                else:
                    top = tile(c, level, pl.ds(pl.multiple_of(core * 16, 8), 8))[7:]
                    bottom = jnp.where(first, tile(c, level, slice(16, 17)), far(c, level))
                front = jnp.where(sub == 0, top, pltpu.roll(centre, 1, 0))
                back = jnp.where(sub == 7, bottom, pltpu.roll(centre, 7, 0))
                total = centre + spread * ((left + right) + (front + back) - 4.0 * centre)
                total = total - u[level] * (right - left) - v[level] * (back - front)
                if level == 0:
                    total = total - wc[0] * q[1]
                elif level == 3:
                    total = total + wc[3] * q[2]
                else:
                    total = total - wc[level] * (q[level + 1] - q[level - 1])
                if c == 2:
                    total = total + (time_step * buoyancy) * tile(3, level, rows)
                elif c == 3:
                    total = total + time_step * w[level]
                gs.append(g[level + 1] * total)
            a = [gs[0]]
            for level in range(1, 4):
                a.append(r[level + 1] * a[-1] + gs[level])
            p = r[5] * a[3]
            part_ref[c, 3, here, :] = a[3]
            b = s[3] * gs[3]
            part_ref[c, 2, here, :] = a[2] + b
            for level in (1, 0):
                b = s[level + 1] * (b + gs[level + 1])
                part_ref[c, level, here, :] = a[level] + b
            b = s[0] * (b + gs[0])
            for block in range(8):
                lanes = slice(128 * block, 128 * block + 128)
                send_ref[8 * half + block, c] = p[:, lanes]
                send_ref[16 + 8 * half + block, c] = b[:, lanes]


def edges_kernel(own_ref, other_ref, far_ref, near_ref, moments_ref, cf_ref, send_ref, mine_ref):
    core = lax.axis_index("core")
    first = core == 0
    for half in range(2):
        rows = pl.ds(pl.multiple_of(core * 16 + 8 * half, 8), 8)
        far, near = far_ref[rows, :], near_ref[rows, :]
        w_low = jnp.where(first, far, near) * -cf_ref[12, 0]
        w_high = jnp.where(first, near, far) * cf_ref[12, 5]
        for c in range(4):
            r = [cf_ref[c, j] for j in range(6)]
            s = [cf_ref[4 + c, j] for j in range(6)]
            lowest = jnp.where(first, own_ref[c, 0, rows, :], other_ref[c, 0, rows, :])
            highest = jnp.where(first, other_ref[c, 1, rows, :], own_ref[c, 1, rows, :])
            low, high = cf_ref[8 + c, 0] * (w_low * lowest), cf_ref[8 + c, 5] * (w_high * highest)
            from_low, from_high = r[1] * low, s[4] * high
            p = (r[2] * r[3] * r[4] * r[5]) * from_low + high
            q = (s[0] * s[1] * s[2] * s[3]) * from_high + low
            for block in range(8):
                lanes = slice(128 * block, 128 * block + 128)
                up, down = 8 * half + block, 16 + 8 * half + block
                send_ref[up, c] = moments_ref[up, c] + p[:, lanes]
                send_ref[down, c] = moments_ref[down, c] + q[:, lanes]
                mine_ref[up, c] = from_low[:, lanes]
                mine_ref[down, c] = from_high[:, lanes]


def scan_kernel(in_ref, cf_ref, out_ref):
    upward = lax.axis_index("y") < 2

    @pl.when(upward)
    def _():
        for c in range(4):
            carry = jnp.zeros((8, 128), jnp.float32)
            for chip in range(32):
                out_ref[chip, c] = carry
                carry = cf_ref[c, 4 * chip + 1] * carry + in_ref[chip, c]

    @pl.when(jnp.logical_not(upward))
    def _():
        for c in range(4):
            carry = jnp.zeros((8, 128), jnp.float32)
            for chip in range(31, -1, -1):
                out_ref[chip, c] = carry
                carry = cf_ref[4 + c, (4 * chip + 127) % 128] * carry + in_ref[chip, c]


def finish_kernel(part_ref, carry_ref, mine_ref, cf_ref, out_ref, send_ref):
    core = lax.axis_index("core")
    for c in range(4):
        r = [cf_ref[c, j] for j in range(6)]
        s = [cf_ref[4 + c, j] for j in range(6)]
        up = [1.0, r[2], r[2] * r[3], r[2] * r[3] * r[4]]
        down = [s[1] * s[2] * s[3], s[2] * s[3], s[3], 1.0]
        for half in range(2):
            here = slice(8 * half, 8 * half + 8)
            rows = pl.ds(pl.multiple_of(core * 16 + 8 * half, 8), 8)
            for block in range(8):
                lanes = slice(128 * block, 128 * block + 128)
                p = carry_ref[8 * half + block, c] + mine_ref[8 * half + block, c]
                q = carry_ref[16 + 8 * half + block, c] + mine_ref[16 + 8 * half + block, c]
                x = [
                    part_ref[c, level, here, lanes] + up[level] * p + down[level] * q
                    for level in range(4)
                ]
                for k in range(2):
                    out_ref[c, k, rows, lanes] = jnp.where(core == 0, x[k], x[2 + k])
                    send_ref[c, k, here, lanes] = jnp.where(core == 0, x[2 + k], x[k])


def shards(flow_state, spacing, diffusivity):
    core = lax.axis_index("core")
    f32 = jnp.float32

    def route(value, axes, sizes, to):
        pairs = []
        for source in range(int(np.prod(sizes))):
            target = to(*(int(i) for i in np.unravel_index(source, sizes)))
            if target is not None:
                pairs.append((source, target))
        return lax.ppermute(value, axes, pairs)

    def across_cores(value):
        return lax.ppermute(value, "core", [(0, 1), (1, 0)])

    def within(chip, k):
        return 2 * chip + k if 0 <= chip < 32 else None

    def to_chip(chip, k):
        return within(chip + 1 if k else chip - 1, 1 - k)

    def to_col(k, z):
        return (1 - k) * 8 + (z + (1 if k else -1)) % 8

    other = across_cores(flow_state)
    edge = lax.dynamic_slice(flow_state, (2, core, 0, 0), (1, 1, 32, 1024)).reshape(32, 1024)
    w_far = route(edge, ROW, (32, 2), to_chip)
    ends = pl.pallas_call(
        ends_kernel,
        out_shape=jax.ShapeDtypeStruct((16, 1024), f32),
        in_specs=[whole()] * 2,
        out_specs=whole(),
        compiler_params=params(),
        name="row_ends",
    )(flow_state, other)
    halo = route(ends, ("core", "zl"), (2, 8), to_col)

    own_cf, scan_cf = pl.pallas_call(
        coefficients_kernel,
        out_shape=(jax.ShapeDtypeStruct((16, 128), f32), jax.ShapeDtypeStruct((8, 128), f32)),
        in_specs=[whole(), whole(pltpu.SMEM)],
        out_specs=(whole(), whole()),
        name="coefficients",
    )(spacing.reshape(1, 128), diffusivity)

    pieces = jax.ShapeDtypeStruct((32, 4, 8, 128), f32)
    part, moments = pl.pallas_call(
        local_kernel,
        out_shape=(jax.ShapeDtypeStruct((4, 4, 16, 1024), f32), pieces),
        in_specs=[whole()] * 3 + [whole(pltpu.SMEM)] * 2,
        out_specs=(whole(), whole()),
        compiler_params=params(),
        name="local_step",
    )(flow_state, other, halo, own_cf, diffusivity)

    w_far, moments, part = lax.optimization_barrier((w_far, moments, part))
    w_near = across_cores(w_far)
    moments, mine = pl.pallas_call(
        edges_kernel,
        out_shape=(pieces, pieces),
        in_specs=[whole()] * 5 + [whole(pltpu.SMEM)],
        out_specs=(whole(), whole()),
        compiler_params=params(),
        name="edge_products",
    )(flow_state, other, w_far, w_near, moments, own_cf)

    arrived = lax.all_to_all(moments, PLANE, split_axis=0, concat_axis=0, tiled=True)
    carried = pl.pallas_call(
        scan_kernel,
        out_shape=pieces,
        in_specs=[whole(), whole(pltpu.SMEM)],
        out_specs=whole(),
        compiler_params=params(),
        name="scan_chips",
    )(arrived, scan_cf)
    returned = lax.all_to_all(carried, PLANE, split_axis=0, concat_axis=0, tiled=True)

    kept, leaving = pl.pallas_call(
        finish_kernel,
        out_shape=(
            jax.ShapeDtypeStruct((4, 2, 32, 1024), f32),
            jax.ShapeDtypeStruct((4, 2, 16, 1024), f32),
        ),
        in_specs=[whole(), whole(), whole(), whole(pltpu.SMEM)],
        out_specs=(whole(), whole()),
        compiler_params=params(),
        name="finish",
    )(part, returned, mine, own_cf)
    back = across_cores(leaving)
    return lax.dynamic_update_slice_in_dim(kept, back, 16 * (1 - core), 2)


def solution(mesh):
    fine = Mesh(mesh.devices.reshape(4, 4, 2, 2, 8), AXES)
    field = P(None, ROW, "zl", None)
    return jax.shard_map(
        shards, mesh=fine, in_specs=(field, P(), P()), out_specs=field, check_vma=False
    )
```

```python
import functools

import jax
import jax.numpy as jnp
import numpy as np
from jax import lax
from jax.experimental import pallas as pl
from jax.experimental.pallas import tpu as pltpu
from jax.sharding import Mesh
from jax.sharding import PartitionSpec as P

time_step = 0.02
cell_width = 0.1
buoyancy = 1.0

AXES = ("y", "x", "zh", "core", "zl")
ROW = AXES[:4]
PLANE = AXES[:3]
LIMIT = 12 * 2**20


def whole(space=pltpu.VMEM):
    return pl.BlockSpec(memory_space=space)


def params():
    return pltpu.CompilerParams(vmem_limit_bytes=LIMIT)


def prefix(matrix, lane, backward):
    a, b, c, d = matrix
    step = 1
    while step < 128:
        by = 128 - step if backward else step
        edge = lane >= 128 - step if backward else lane < step
        pa, pb, pc, pd = (pltpu.roll(m, by, 1) for m in (a, b, c, d))
        pa, pb = jnp.where(edge, 1.0, pa), jnp.where(edge, 0.0, pb)
        pc, pd = jnp.where(edge, 0.0, pc), jnp.where(edge, 1.0, pd)
        a, b, c, d = a * pa + b * pc, a * pb + b * pd, c * pa + d * pc, c * pb + d * pd
        scale = 1.0 / (a + b + c + d)
        a, b, c, d = a * scale, b * scale, c * scale, d * scale
        step *= 2
    return (a + b) / (c + d)


def chip_index():
    return (lax.axis_index("y") * 4 + lax.axis_index("x")) * 2 + lax.axis_index("zh")


def coefficients_kernel(spacing_ref, diffusivity_ref, own_ref, scan_ref):
    shape = (8, 128)
    lane = lax.broadcasted_iota(jnp.int32, shape, 1)
    row = lax.broadcasted_iota(jnp.int32, shape, 0)
    below = jnp.broadcast_to(spacing_ref[...], shape)
    above = jnp.where(lane == 127, below, pltpu.roll(below, 127, 1))
    across = below + above
    rate = jnp.full(shape, diffusivity_ref[3], jnp.float32)
    for component in range(3):
        rate = jnp.where(row % 4 == component, diffusivity_ref[component], rate)
    rate = time_step * rate
    low, up = 2.0 * rate / (across * below), 2.0 * rate / (across * above)
    up_before = jnp.where(lane == 0, 0.0, pltpu.roll(up, 1, 1))
    low_after = jnp.where(lane == 127, 0.0, pltpu.roll(low, 127, 1))
    one = jnp.ones(shape, jnp.float32)
    t = prefix((1.0 + low, up_before, one, up_before), lane, False)
    tau = prefix((1.0 + up, low_after, one, low_after), lane, True)
    r = jnp.where(lane == 0, 0.0, low / (low + tau))
    s = jnp.where(lane == 127, 0.0, up / (up + t))
    g = 1.0 / (t + tau - 1.0)
    rs = jnp.where(row < 4, r, s)
    gc = jnp.where(row < 4, g, time_step / across)
    four = rs * pltpu.roll(rs, 127, 1)
    four = four * pltpu.roll(four, 126, 1)
    scan_ref[...] = four * pltpu.roll(four, 124, 1)
    turn = lax.rem(129 - 4 * chip_index(), 128)
    own_ref[0:8, :] = pltpu.roll(rs, turn, 1)
    own_ref[8:16, :] = pltpu.roll(gc, turn, 1)
    own_ref[16:24, :] = pltpu.roll(four, turn, 1)


def pair_factors(cf_ref, c):
    lower = lax.axis_index("zh") == 0
    r0 = jnp.where(lower, cf_ref[16 + c, 2], cf_ref[16 + c, 126])
    r1 = jnp.where(lower, cf_ref[16 + c, 6], cf_ref[16 + c, 2])
    s0 = jnp.where(lower, cf_ref[20 + c, 0], cf_ref[20 + c, 124])
    s1 = jnp.where(lower, cf_ref[20 + c, 4], cf_ref[20 + c, 0])
    return lower, r0, r1, s0, s1


def piece(half, block, down):
    return 8 * down + 4 * half + block // 2


def ends_kernel(own_ref, other_ref, out_ref):
    first = lax.axis_index("core") == 0
    for line in range(8):
        c, k = line // 2, line % 2
        for at, ref in ((line, own_ref), (8 + line, other_ref)):
            out_ref[at : at + 1, :] = jnp.where(first, ref[c, k, 0:1, :], ref[c, k, 31:32, :])


def local_kernel(own_ref, other_ref, halo_ref, cf_ref, dif_ref, part_ref, *send_refs):
    core = lax.axis_index("core")
    first = core == 0
    sub = lax.broadcasted_iota(jnp.int32, (8, 1024), 0)
    rate = time_step / (2.0 * cell_width)

    def tile(c, level, rows):
        return jnp.where(
            core == level // 2, own_ref[c, level % 2, rows, :], other_ref[c, level % 2, rows, :]
        )

    def far(c, level):
        line = 2 * c + level % 2
        return jnp.where(
            core == level // 2, halo_ref[8 + line : 9 + line, :], halo_ref[line : line + 1, :]
        )

    for half in range(2):
        rows = pl.ds(pl.multiple_of(core * 16 + 8 * half, 8), 8)
        here = slice(8 * half, 8 * half + 8)
        u = [tile(0, level, rows) * rate for level in range(4)]
        v = [tile(1, level, rows) * rate for level in range(4)]
        w = [tile(2, level, rows) for level in range(4)]
        wc = [w[level] * cf_ref[12, level + 1] for level in range(4)]
        for c in range(4):
            r = [cf_ref[c, j] for j in range(6)]
            s = [cf_ref[4 + c, j] for j in range(6)]
            g = [cf_ref[8 + c, j] for j in range(6)]
            spread = dif_ref[c] * (time_step / cell_width**2)
            q = w if c == 2 else [tile(c, level, rows) for level in range(4)]
            gs = []
            for level in range(4):
                centre = q[level]
                left, right = pltpu.roll(centre, 1, 1), pltpu.roll(centre, 1023, 1)
                if half == 0:
                    top = jnp.where(first, far(c, level), tile(c, level, slice(15, 16)))
                    bottom = tile(c, level, pl.ds(pl.multiple_of(core * 16 + 8, 8), 8))[:1]
                else:
                    top = tile(c, level, pl.ds(pl.multiple_of(core * 16, 8), 8))[7:]
                    bottom = jnp.where(first, tile(c, level, slice(16, 17)), far(c, level))
                front = jnp.where(sub == 0, top, pltpu.roll(centre, 1, 0))
                back = jnp.where(sub == 7, bottom, pltpu.roll(centre, 7, 0))
                total = centre + spread * ((left + right) + (front + back) - 4.0 * centre)
                total = total - u[level] * (right - left) - v[level] * (back - front)
                if level == 0:
                    total = total - wc[0] * q[1]
                elif level == 3:
                    total = total + wc[3] * q[2]
                else:
                    total = total - wc[level] * (q[level + 1] - q[level - 1])
                if c == 2:
                    total = total + (time_step * buoyancy) * tile(3, level, rows)
                elif c == 3:
                    total = total + time_step * w[level]
                gs.append(g[level + 1] * total)
            a = [gs[0]]
            for level in range(1, 4):
                a.append(r[level + 1] * a[-1] + gs[level])
            p = r[5] * a[3]
            part_ref[c, 3, here, :] = a[3]
            b = s[3] * gs[3]
            part_ref[c, 2, here, :] = a[2] + b
            for level in (1, 0):
                b = s[level + 1] * (b + gs[level + 1])
                part_ref[c, level, here, :] = a[level] + b
            b = s[0] * (b + gs[0])
            for block in range(8):
                lanes = slice(128 * block, 128 * block + 128)
                send_refs[c // 2][piece(half, block, 0), c % 2, block % 2] = p[:, lanes]
                send_refs[c // 2][piece(half, block, 1), c % 2, block % 2] = b[:, lanes]


def edges_kernel(
    own_ref, other_ref, far_ref, near_ref, raw01_ref, raw23_ref, cf_ref,
    sum01_ref, sum23_ref, scaled_ref, mine01_ref, mine23_ref,
):
    core = lax.axis_index("core")
    first = core == 0
    for half in range(2):
        rows = pl.ds(pl.multiple_of(core * 16 + 8 * half, 8), 8)
        far, near = far_ref[rows, :], near_ref[rows, :]
        w_low = jnp.where(first, far, near) * -cf_ref[12, 0]
        w_high = jnp.where(first, near, far) * cf_ref[12, 5]
        for c in range(4):
            raw_ref, sum_ref, mine_ref = (
                (raw01_ref, sum01_ref, mine01_ref),
                (raw23_ref, sum23_ref, mine23_ref),
            )[c // 2]
            lower, _, r1, s0, _ = pair_factors(cf_ref, c)
            r = [cf_ref[c, j] for j in range(6)]
            s = [cf_ref[4 + c, j] for j in range(6)]
            lowest = jnp.where(first, own_ref[c, 0, rows, :], other_ref[c, 0, rows, :])
            highest = jnp.where(first, other_ref[c, 1, rows, :], own_ref[c, 1, rows, :])
            low, high = cf_ref[8 + c, 0] * (w_low * lowest), cf_ref[8 + c, 5] * (w_high * highest)
            from_low, from_high = r[1] * low, s[4] * high
            p = (r[2] * r[3] * r[4] * r[5]) * from_low + high
            q = (s[0] * s[1] * s[2] * s[3]) * from_high + low
            for block in range(8):
                lanes = slice(128 * block, 128 * block + 128)
                up = piece(half, block, 0), c % 2, block % 2
                down = piece(half, block, 1), c % 2, block % 2
                total_p, total_q = raw_ref[up] + p[:, lanes], raw_ref[down] + q[:, lanes]
                sum_ref[up] = total_p
                sum_ref[down] = total_q
                mine_ref[up] = from_low[:, lanes]
                mine_ref[down] = from_high[:, lanes]
                if c >= 2:
                    scaled_ref[up] = jnp.where(lower, r1, 1.0) * total_p
                    scaled_ref[down] = jnp.where(lower, 1.0, s0) * total_q


def pair_kernel(own_ref, partner_ref, cf_ref, out_ref):
    for c in range(2):
        lower, _, r1, s0, _ = pair_factors(cf_ref, c)
        own_p, partner_p = jnp.where(lower, r1, 1.0), jnp.where(lower, 1.0, r1)
        own_q, partner_q = jnp.where(lower, 1.0, s0), jnp.where(lower, s0, 1.0)
        out_ref[0:8, c] = own_p * own_ref[0:8, c] + partner_p * partner_ref[0:8, c]
        out_ref[8:16, c] = own_q * own_ref[8:16, c] + partner_q * partner_ref[8:16, c]


def scan_kernel(base, in_ref, cf_ref, out_ref):
    upward = lax.axis_index("y") < 2

    @pl.when(upward)
    def _():
        for c in range(2):
            carry = jnp.zeros((2, 8, 128), jnp.float32)
            for pair in range(16):
                out_ref[pair, c] = carry
                carry = cf_ref[base + c, 8 * pair + 1] * carry + in_ref[pair, c]

    @pl.when(jnp.logical_not(upward))
    def _():
        for c in range(2):
            carry = jnp.zeros((2, 8, 128), jnp.float32)
            for pair in range(15, -1, -1):
                out_ref[pair, c] = carry
                carry = cf_ref[4 + base + c, (8 * pair + 127) % 128] * carry + in_ref[pair, c]


def crossing_kernel(own_ref, carry_ref, cf_ref, out_ref):
    for c in range(2):
        lower, r0, _, _, s1 = pair_factors(cf_ref, 2 + c)
        up, down = carry_ref[0:8, c], carry_ref[8:16, c]
        out_ref[0:8, c] = jnp.where(lower, r0 * up + own_ref[0:8, c], up)
        out_ref[8:16, c] = jnp.where(lower, down, s1 * down + own_ref[8:16, c])


def finish_kernel(
    part_ref, carry01_ref, partner01_ref, mine01_ref, carry23_ref, partner23_ref, mine23_ref,
    cf_ref, out_ref, send_ref,
):
    core = lax.axis_index("core")
    for c in range(4):
        carry_ref, partner_ref, mine_ref = (
            (carry01_ref, partner01_ref, mine01_ref),
            (carry23_ref, partner23_ref, mine23_ref),
        )[c // 2]
        lower, r0, _, _, s1 = pair_factors(cf_ref, c)
        by_p, by_q = jnp.where(lower, 1.0, r0), jnp.where(lower, s1, 1.0)
        r = [cf_ref[c, j] for j in range(6)]
        s = [cf_ref[4 + c, j] for j in range(6)]
        rise = [1.0, r[2], r[2] * r[3], r[2] * r[3] * r[4]]
        fall = [s[1] * s[2] * s[3], s[2] * s[3], s[3], 1.0]
        for half in range(2):
            here = slice(8 * half, 8 * half + 8)
            rows = pl.ds(pl.multiple_of(core * 16 + 8 * half, 8), 8)
            for block in range(8):
                lanes = slice(128 * block, 128 * block + 128)
                up = piece(half, block, 0), c % 2, block % 2
                down = piece(half, block, 1), c % 2, block % 2
                p = by_p * carry_ref[up] + mine_ref[up]
                q = by_q * carry_ref[down] + mine_ref[down]
                if c < 2:
                    p = p + jnp.where(lower, 0.0, partner_ref[up])
                    q = q + jnp.where(lower, partner_ref[down], 0.0)
                else:
                    p, q = p + partner_ref[up], q + partner_ref[down]
                x = [
                    part_ref[c, level, here, lanes] + rise[level] * p + fall[level] * q
                    for level in range(4)
                ]
                for k in range(2):
                    out_ref[c, k, rows, lanes] = jnp.where(core == 0, x[k], x[2 + k])
                    send_ref[c, k, here, lanes] = jnp.where(core == 0, x[2 + k], x[k])


def shards(flow_state, spacing, diffusivity):
    core = lax.axis_index("core")
    f32 = jnp.float32

    def route(value, axes, sizes, to):
        pairs = []
        for source in range(int(np.prod(sizes))):
            target = to(*(int(i) for i in np.unravel_index(source, sizes)))
            if target is not None:
                pairs.append((source, target))
        return lax.ppermute(value, axes, pairs)

    def across_cores(value):
        return lax.ppermute(value, "core", [(0, 1), (1, 0)])

    def within(chip, k):
        return 2 * chip + k if 0 <= chip < 32 else None

    def to_chip(chip, k):
        return within(chip + 1 if k else chip - 1, 1 - k)

    def to_col(k, z):
        return (1 - k) * 8 + (z + (1 if k else -1)) % 8

    other = across_cores(flow_state)
    edge = lax.dynamic_slice(flow_state, (2, core, 0, 0), (1, 1, 32, 1024)).reshape(32, 1024)
    w_far = route(edge, ROW, (32, 2), to_chip)
    ends = pl.pallas_call(
        ends_kernel,
        out_shape=jax.ShapeDtypeStruct((16, 1024), f32),
        in_specs=[whole()] * 2,
        out_specs=whole(),
        compiler_params=params(),
        name="row_ends",
    )(flow_state, other)
    halo = route(ends, ("core", "zl"), (2, 8), to_col)

    own_cf, scan_cf = pl.pallas_call(
        coefficients_kernel,
        out_shape=(jax.ShapeDtypeStruct((24, 128), f32), jax.ShapeDtypeStruct((8, 128), f32)),
        in_specs=[whole(), whole(pltpu.SMEM)],
        out_specs=(whole(), whole()),
        name="coefficients",
    )(spacing.reshape(1, 128), diffusivity)

    def call(kernel, name, outs, *args):
        smem = {id(own_cf), id(scan_cf), id(diffusivity)}
        return pl.pallas_call(
            kernel,
            out_shape=outs,
            in_specs=[whole(pltpu.SMEM if id(a) in smem else pltpu.VMEM) for a in args],
            out_specs=jax.tree.map(lambda _: whole(), outs),
            compiler_params=params(),
            name=name,
        )(*args)

    def in_plane(value):
        return lax.all_to_all(value, ("y", "x"), split_axis=0, concat_axis=0, tiled=True)

    def to_partner(value):
        return lax.ppermute(value, "zh", [(0, 1), (1, 0)])

    def scanned(value, base):
        kernel = functools.partial(scan_kernel, base)
        return in_plane(call(kernel, "scan_pairs", pieces, in_plane(value), scan_cf))

    def array(*shape):
        return jax.ShapeDtypeStruct(shape, f32)

    pieces = array(16, 2, 2, 8, 128)
    halo, w_far, own_cf, scan_cf = lax.optimization_barrier((halo, w_far, own_cf, scan_cf))
    w_near = across_cores(w_far)
    part, raw01, raw23 = call(
        local_kernel,
        "local_step",
        (array(4, 4, 16, 1024), pieces, pieces),
        flow_state, other, halo, own_cf, diffusivity,
    )
    sum01, sum23, scaled, mine01, mine23 = call(
        edges_kernel,
        "edge_products",
        (pieces,) * 5,
        flow_state, other, w_far, w_near, raw01, raw23, own_cf,
    )

    partner01 = to_partner(sum01)
    carry23 = scanned(scaled, 2)
    leaving23 = call(crossing_kernel, "crossing", pieces, sum23, carry23, own_cf)
    partner01, leaving23 = lax.optimization_barrier((partner01, leaving23))
    partner23 = to_partner(leaving23)
    carry01 = scanned(call(pair_kernel, "pair_moments", pieces, sum01, partner01, own_cf), 0)
    kept, leaving = call(
        finish_kernel,
        "finish",
        (array(4, 2, 32, 1024), array(4, 2, 16, 1024)),
        part, carry01, partner01, mine01, carry23, partner23, mine23, own_cf,
    )
    back = across_cores(leaving)
    return lax.dynamic_update_slice_in_dim(kept, back, 16 * (1 - core), 2)


def solution(mesh):
    fine = Mesh(mesh.devices.reshape(4, 4, 2, 2, 8), AXES)
    field = P(None, ROW, "zl", None)
    return jax.shard_map(
        shards, mesh=fine, in_specs=(field, P(), P()), out_specs=field, check_vma=False
    )
```

```python
import functools

import jax
import jax.numpy as jnp
import numpy as np
from jax import lax
from jax.experimental import pallas as pl
from jax.experimental.pallas import tpu as pltpu
from jax.sharding import Mesh
from jax.sharding import PartitionSpec as P

time_step = 0.02
cell_width = 0.1
buoyancy = 1.0

AXES = ("y", "x", "zh", "core", "zl")
ROW = AXES[:4]
PLANE = AXES[:3]
LIMIT = 12 * 2**20


def whole(space=pltpu.VMEM):
    return pl.BlockSpec(memory_space=space)


def params():
    return pltpu.CompilerParams(vmem_limit_bytes=LIMIT)


def prefix(matrix, lane, backward):
    a, b, c, d = matrix
    step = 1
    while step < 128:
        by = 128 - step if backward else step
        edge = lane >= 128 - step if backward else lane < step
        pa, pb, pc, pd = (pltpu.roll(m, by, 1) for m in (a, b, c, d))
        pa, pb = jnp.where(edge, 1.0, pa), jnp.where(edge, 0.0, pb)
        pc, pd = jnp.where(edge, 0.0, pc), jnp.where(edge, 1.0, pd)
        a, b, c, d = a * pa + b * pc, a * pb + b * pd, c * pa + d * pc, c * pb + d * pd
        scale = 1.0 / (a + b + c + d)
        a, b, c, d = a * scale, b * scale, c * scale, d * scale
        step *= 2
    return (a + b) / (c + d)


def chip_index():
    return (lax.axis_index("y") * 4 + lax.axis_index("x")) * 2 + lax.axis_index("zh")


def coefficients_kernel(spacing_ref, diffusivity_ref, own_ref, scan_ref):
    shape = (8, 128)
    lane = lax.broadcasted_iota(jnp.int32, shape, 1)
    row = lax.broadcasted_iota(jnp.int32, shape, 0)
    below = jnp.broadcast_to(spacing_ref[...], shape)
    above = jnp.where(lane == 127, below, pltpu.roll(below, 127, 1))
    across = below + above
    rate = jnp.full(shape, diffusivity_ref[3], jnp.float32)
    for component in range(3):
        rate = jnp.where(row % 4 == component, diffusivity_ref[component], rate)
    rate = time_step * rate
    low, up = 2.0 * rate / (across * below), 2.0 * rate / (across * above)
    up_before = jnp.where(lane == 0, 0.0, pltpu.roll(up, 1, 1))
    low_after = jnp.where(lane == 127, 0.0, pltpu.roll(low, 127, 1))
    one = jnp.ones(shape, jnp.float32)
    t = prefix((1.0 + low, up_before, one, up_before), lane, False)
    tau = prefix((1.0 + up, low_after, one, low_after), lane, True)
    r = jnp.where(lane == 0, 0.0, low / (low + tau))
    s = jnp.where(lane == 127, 0.0, up / (up + t))
    g = 1.0 / (t + tau - 1.0)
    rs = jnp.where(row < 4, r, s)
    gc = jnp.where(row < 4, g, time_step / across)
    four = rs * pltpu.roll(rs, 127, 1)
    four = four * pltpu.roll(four, 126, 1)
    scan_ref[0:8, :] = four * pltpu.roll(four, 124, 1)
    scan_ref[8:16, :] = four
    turn = lax.rem(129 - 4 * chip_index(), 128)
    own_ref[0:8, :] = pltpu.roll(rs, turn, 1)
    own_ref[8:16, :] = pltpu.roll(gc, turn, 1)
    own_ref[16:24, :] = pltpu.roll(four, turn, 1)


def pair_factors(cf_ref, c):
    lower = lax.axis_index("zh") == 0
    r0 = jnp.where(lower, cf_ref[16 + c, 2], cf_ref[16 + c, 126])
    r1 = jnp.where(lower, cf_ref[16 + c, 6], cf_ref[16 + c, 2])
    s0 = jnp.where(lower, cf_ref[20 + c, 0], cf_ref[20 + c, 124])
    s1 = jnp.where(lower, cf_ref[20 + c, 4], cf_ref[20 + c, 0])
    return lower, r0, r1, s0, s1


def piece(half, block, down):
    return 8 * down + 4 * half + block // 2


def ends_kernel(own_ref, other_ref, out_ref):
    first = lax.axis_index("core") == 0
    for line in range(8):
        c, k = line // 2, line % 2
        for at, ref in ((line, own_ref), (8 + line, other_ref)):
            out_ref[at : at + 1, :] = jnp.where(first, ref[c, k, 0:1, :], ref[c, k, 31:32, :])


def local_kernel(own_ref, other_ref, halo_ref, cf_ref, dif_ref, part_ref, *send_refs):
    core = lax.axis_index("core")
    first = core == 0
    sub = lax.broadcasted_iota(jnp.int32, (8, 1024), 0)
    rate = time_step / (2.0 * cell_width)

    def tile(c, level, rows):
        return jnp.where(
            core == level // 2, own_ref[c, level % 2, rows, :], other_ref[c, level % 2, rows, :]
        )

    def far(c, level):
        line = 2 * c + level % 2
        return jnp.where(
            core == level // 2, halo_ref[8 + line : 9 + line, :], halo_ref[line : line + 1, :]
        )

    for half in range(2):
        rows = pl.ds(pl.multiple_of(core * 16 + 8 * half, 8), 8)
        here = slice(8 * half, 8 * half + 8)
        u = [tile(0, level, rows) * rate for level in range(4)]
        v = [tile(1, level, rows) * rate for level in range(4)]
        w = [tile(2, level, rows) for level in range(4)]
        wc = [w[level] * cf_ref[12, level + 1] for level in range(4)]
        for c in range(4):
            r = [cf_ref[c, j] for j in range(6)]
            s = [cf_ref[4 + c, j] for j in range(6)]
            g = [cf_ref[8 + c, j] for j in range(6)]
            spread = dif_ref[c] * (time_step / cell_width**2)
            q = w if c == 2 else [tile(c, level, rows) for level in range(4)]
            gs = []
            for level in range(4):
                centre = q[level]
                left, right = pltpu.roll(centre, 1, 1), pltpu.roll(centre, 1023, 1)
                if half == 0:
                    top = jnp.where(first, far(c, level), tile(c, level, slice(15, 16)))
                    bottom = tile(c, level, pl.ds(pl.multiple_of(core * 16 + 8, 8), 8))[:1]
                else:
                    top = tile(c, level, pl.ds(pl.multiple_of(core * 16, 8), 8))[7:]
                    bottom = jnp.where(first, tile(c, level, slice(16, 17)), far(c, level))
                front = jnp.where(sub == 0, top, pltpu.roll(centre, 1, 0))
                back = jnp.where(sub == 7, bottom, pltpu.roll(centre, 7, 0))
                total = centre + spread * ((left + right) + (front + back) - 4.0 * centre)
                total = total - u[level] * (right - left) - v[level] * (back - front)
                if level == 0:
                    total = total - wc[0] * q[1]
                elif level == 3:
                    total = total + wc[3] * q[2]
                else:
                    total = total - wc[level] * (q[level + 1] - q[level - 1])
                if c == 2:
                    total = total + (time_step * buoyancy) * tile(3, level, rows)
                elif c == 3:
                    total = total + time_step * w[level]
                gs.append(g[level + 1] * total)
            a = [gs[0]]
            for level in range(1, 4):
                a.append(r[level + 1] * a[-1] + gs[level])
            p = r[5] * a[3]
            part_ref[c, 3, here, :] = a[3]
            b = s[3] * gs[3]
            part_ref[c, 2, here, :] = a[2] + b
            for level in (1, 0):
                b = s[level + 1] * (b + gs[level + 1])
                part_ref[c, level, here, :] = a[level] + b
            b = s[0] * (b + gs[0])
            for block in range(8):
                lanes = slice(128 * block, 128 * block + 128)
                send_refs[c // 2][piece(half, block, 0), c % 2, block % 2] = p[:, lanes]
                send_refs[c // 2][piece(half, block, 1), c % 2, block % 2] = b[:, lanes]


def weights(cf_ref, c):
    r = [cf_ref[c, j] for j in range(6)]
    s = [cf_ref[4 + c, j] for j in range(6)]
    rise = [1.0, r[2], r[2] * r[3], r[2] * r[3] * r[4]]
    return rise, [s[1] * s[2] * s[3], s[2] * s[3], s[3], 1.0]


def edges_kernel(
    own_ref, other_ref, far_ref, near_ref, raw01_ref, raw23_ref, old_ref, cf_ref,
    sum01_ref, sum23_ref, part_ref,
):
    core = lax.axis_index("core")
    first = core == 0
    for half in range(2):
        rows = pl.ds(pl.multiple_of(core * 16 + 8 * half, 8), 8)
        far, near = far_ref[rows, :], near_ref[rows, :]
        w_low = jnp.where(first, far, near) * -cf_ref[12, 0]
        w_high = jnp.where(first, near, far) * cf_ref[12, 5]
        for c in range(4):
            raw_ref, sum_ref = ((raw01_ref, sum01_ref), (raw23_ref, sum23_ref))[c // 2]
            r = [cf_ref[c, j] for j in range(6)]
            s = [cf_ref[4 + c, j] for j in range(6)]
            lowest = jnp.where(first, own_ref[c, 0, rows, :], other_ref[c, 0, rows, :])
            highest = jnp.where(first, other_ref[c, 1, rows, :], own_ref[c, 1, rows, :])
            low, high = cf_ref[8 + c, 0] * (w_low * lowest), cf_ref[8 + c, 5] * (w_high * highest)
            from_low, from_high = r[1] * low, s[4] * high
            p = (r[2] * r[3] * r[4] * r[5]) * from_low + high
            q = (s[0] * s[1] * s[2] * s[3]) * from_high + low
            for block in range(8):
                lanes = slice(128 * block, 128 * block + 128)
                up = piece(half, block, 0), c % 2, block % 2
                down = piece(half, block, 1), c % 2, block % 2
                sum_ref[up] = raw_ref[up] + p[:, lanes]
                sum_ref[down] = raw_ref[down] + q[:, lanes]
            rise, fall = weights(cf_ref, c)
            here = slice(8 * half, 8 * half + 8)
            for level in range(4):
                part_ref[c, level, here, :] = old_ref[c, level, here, :] + (
                    rise[level] * from_low + fall[level] * from_high
                )


def pair_kernel(own_ref, partner_ref, cf_ref, out_ref):
    for c in range(2):
        lower, _, r1, s0, _ = pair_factors(cf_ref, c)
        own_p, partner_p = jnp.where(lower, r1, 1.0), jnp.where(lower, 1.0, r1)
        own_q, partner_q = jnp.where(lower, 1.0, s0), jnp.where(lower, s0, 1.0)
        out_ref[0:8, c] = own_p * own_ref[0:8, c] + partner_p * partner_ref[0:8, c]
        out_ref[8:16, c] = own_q * own_ref[8:16, c] + partner_q * partner_ref[8:16, c]


def scan_kernel(base, in_ref, cf_ref, out_ref):
    upward = lax.axis_index("y") < 2
    lower = lax.axis_index("zh") == 0

    def scaled(pair, c, at, by):
        value = in_ref[pair, c]
        return value if base == 0 else jnp.where(by, cf_ref[8 + at, (8 * pair + 5 if at < 4 else 8 * pair + 127) % 128], 1.0) * value

    @pl.when(upward)
    def _():
        for c in range(2):
            carry = jnp.zeros((2, 8, 128), jnp.float32)
            for pair in range(16):
                out_ref[pair, c] = carry
                carry = cf_ref[base + c, 8 * pair + 1] * carry + scaled(pair, c, base + c, lower)

    @pl.when(jnp.logical_not(upward))
    def _():
        for c in range(2):
            carry = jnp.zeros((2, 8, 128), jnp.float32)
            for pair in range(15, -1, -1):
                out_ref[pair, c] = carry
                at = 4 + base + c
                kept = cf_ref[at, (8 * pair + 127) % 128] * carry
                carry = kept + scaled(pair, c, at, jnp.logical_not(lower))


def crossing_kernel(own_ref, carry_ref, cf_ref, out_ref):
    for c in range(2):
        lower, r0, _, _, s1 = pair_factors(cf_ref, 2 + c)
        up, down = carry_ref[0:8, c], carry_ref[8:16, c]
        out_ref[0:8, c] = jnp.where(lower, r0 * up + own_ref[0:8, c], up)
        out_ref[8:16, c] = jnp.where(lower, down, s1 * down + own_ref[8:16, c])


def finish_kernel(
    part_ref, carry01_ref, partner01_ref, carry23_ref, partner23_ref, cf_ref, out_ref, send_ref
):
    core = lax.axis_index("core")
    for c in range(4):
        carry_ref, partner_ref = (
            (carry01_ref, partner01_ref),
            (carry23_ref, partner23_ref),
        )[c // 2]
        lower, r0, _, _, s1 = pair_factors(cf_ref, c)
        by_p, by_q = jnp.where(lower, 1.0, r0), jnp.where(lower, s1, 1.0)
        rise, fall = weights(cf_ref, c)
        for half in range(2):
            here = slice(8 * half, 8 * half + 8)
            rows = pl.ds(pl.multiple_of(core * 16 + 8 * half, 8), 8)
            for block in range(8):
                lanes = slice(128 * block, 128 * block + 128)
                up = piece(half, block, 0), c % 2, block % 2
                down = piece(half, block, 1), c % 2, block % 2
                p = by_p * carry_ref[up]
                q = by_q * carry_ref[down]
                if c < 2:
                    p = p + jnp.where(lower, 0.0, partner_ref[up])
                    q = q + jnp.where(lower, partner_ref[down], 0.0)
                else:
                    p, q = p + partner_ref[up], q + partner_ref[down]
                x = [
                    part_ref[c, level, here, lanes] + rise[level] * p + fall[level] * q
                    for level in range(4)
                ]
                for k in range(2):
                    out_ref[c, k, rows, lanes] = jnp.where(core == 0, x[k], x[2 + k])
                    send_ref[c, k, here, lanes] = jnp.where(core == 0, x[2 + k], x[k])


def shards(flow_state, spacing, diffusivity):
    core = lax.axis_index("core")
    f32 = jnp.float32

    def route(value, axes, sizes, to):
        pairs = []
        for source in range(int(np.prod(sizes))):
            target = to(*(int(i) for i in np.unravel_index(source, sizes)))
            if target is not None:
                pairs.append((source, target))
        return lax.ppermute(value, axes, pairs)

    def across_cores(value):
        return lax.ppermute(value, "core", [(0, 1), (1, 0)])

    def within(chip, k):
        return 2 * chip + k if 0 <= chip < 32 else None

    def to_chip(chip, k):
        return within(chip + 1 if k else chip - 1, 1 - k)

    def to_col(k, z):
        return (1 - k) * 8 + (z + (1 if k else -1)) % 8

    other = across_cores(flow_state)
    edge = lax.dynamic_slice(flow_state, (2, core, 0, 0), (1, 1, 32, 1024)).reshape(32, 1024)
    w_far = route(edge, ROW, (32, 2), to_chip)
    ends = pl.pallas_call(
        ends_kernel,
        out_shape=jax.ShapeDtypeStruct((16, 1024), f32),
        in_specs=[whole()] * 2,
        out_specs=whole(),
        compiler_params=params(),
        name="row_ends",
    )(flow_state, other)
    halo = route(ends, ("core", "zl"), (2, 8), to_col)

    own_cf, scan_cf = pl.pallas_call(
        coefficients_kernel,
        out_shape=(jax.ShapeDtypeStruct((24, 128), f32), jax.ShapeDtypeStruct((16, 128), f32)),
        in_specs=[whole(), whole(pltpu.SMEM)],
        out_specs=(whole(), whole()),
        compiler_params=params(),
        name="coefficients",
    )(spacing.reshape(1, 128), diffusivity)

    def call(kernel, name, outs, *args, **more):
        smem = {id(own_cf), id(scan_cf), id(diffusivity)}
        return pl.pallas_call(
            kernel,
            out_shape=outs,
            in_specs=[whole(pltpu.SMEM if id(a) in smem else pltpu.VMEM) for a in args],
            out_specs=jax.tree.map(lambda _: whole(), outs),
            compiler_params=params(),
            name=name,
            **more,
        )(*args)

    def in_plane(value):
        return lax.all_to_all(value, ("y", "x"), split_axis=0, concat_axis=0, tiled=True)

    def to_partner(value):
        return lax.ppermute(value, "zh", [(0, 1), (1, 0)])

    def scanned(value, base):
        kernel = functools.partial(scan_kernel, base)
        return in_plane(call(kernel, "scan_pairs", pieces, in_plane(value), scan_cf))

    def array(*shape):
        return jax.ShapeDtypeStruct(shape, f32)

    pieces = array(16, 2, 2, 8, 128)
    halo, w_far, own_cf, scan_cf = lax.optimization_barrier((halo, w_far, own_cf, scan_cf))
    w_near = across_cores(w_far)
    part, raw01, raw23 = call(
        local_kernel,
        "local_step",
        (array(4, 4, 16, 1024), pieces, pieces),
        flow_state, other, halo, own_cf, diffusivity,
    )
    sum01, sum23, part = call(
        edges_kernel,
        "edge_products",
        (pieces, pieces, array(4, 4, 16, 1024)),
        flow_state, other, w_far, w_near, raw01, raw23, part, own_cf,
        input_output_aliases={4: 0, 5: 1, 6: 2},
    )

    partner01 = to_partner(sum01)
    once = lax.optimization_barrier(jnp.int32(1))
    carry23 = lax.fori_loop(0, once, lambda _, value: scanned(value, 2), sum23)
    leaving23 = call(crossing_kernel, "crossing", pieces, sum23, carry23, own_cf)
    partner23 = to_partner(leaving23)

    def scan_pairs01(_, value):
        return scanned(call(pair_kernel, "pair_moments", pieces, value, partner01, own_cf), 0)

    sum01, _ = lax.optimization_barrier((sum01, leaving23))
    carry01 = lax.fori_loop(0, once, scan_pairs01, sum01)
    kept, leaving = call(
        finish_kernel,
        "finish",
        (array(4, 2, 32, 1024), array(4, 2, 16, 1024)),
        part, carry01, partner01, carry23, partner23, own_cf,
    )
    back = across_cores(leaving)
    return lax.dynamic_update_slice_in_dim(kept, back, 16 * (1 - core), 2)


def solution(mesh):
    fine = Mesh(mesh.devices.reshape(4, 4, 2, 2, 8), AXES)
    field = P(None, ROW, "zl", None)
    return jax.shard_map(
        shards, mesh=fine, in_specs=(field, P(), P()), out_specs=field, check_vma=False
    )
```

```python
import functools

import jax
import jax.numpy as jnp
import numpy as np
from jax import lax
from jax.experimental import pallas as pl
from jax.experimental.pallas import tpu as pltpu
from jax.sharding import Mesh
from jax.sharding import PartitionSpec as P

time_step = 0.02
cell_width = 0.1
buoyancy = 1.0

AXES = ("y", "x", "zh", "core", "zl")
ROW = AXES[:4]
PLANE = AXES[:3]
LIMIT = 12 * 2**20


def whole(space=pltpu.VMEM):
    return pl.BlockSpec(memory_space=space)


def params():
    return pltpu.CompilerParams(vmem_limit_bytes=LIMIT)


def prefix(matrix, lane, backward):
    a, b, c, d = matrix
    step = 1
    while step < 128:
        by = 128 - step if backward else step
        edge = lane >= 128 - step if backward else lane < step
        pa, pb, pc, pd = (pltpu.roll(m, by, 1) for m in (a, b, c, d))
        pa, pb = jnp.where(edge, 1.0, pa), jnp.where(edge, 0.0, pb)
        pc, pd = jnp.where(edge, 0.0, pc), jnp.where(edge, 1.0, pd)
        a, b, c, d = a * pa + b * pc, a * pb + b * pd, c * pa + d * pc, c * pb + d * pd
        scale = 1.0 / (a + b + c + d)
        a, b, c, d = a * scale, b * scale, c * scale, d * scale
        step *= 2
    return (a + b) / (c + d)


def chip_index():
    return (lax.axis_index("y") * 4 + lax.axis_index("x")) * 2 + lax.axis_index("zh")


def coefficients_kernel(spacing_ref, diffusivity_ref, own_ref, scan_ref):
    shape = (8, 128)
    lane = lax.broadcasted_iota(jnp.int32, shape, 1)
    row = lax.broadcasted_iota(jnp.int32, shape, 0)
    below = jnp.broadcast_to(spacing_ref[...], shape)
    above = jnp.where(lane == 127, below, pltpu.roll(below, 127, 1))
    across = below + above
    rate = jnp.full(shape, diffusivity_ref[3], jnp.float32)
    for component in range(3):
        rate = jnp.where(row % 4 == component, diffusivity_ref[component], rate)
    rate = time_step * rate
    low, up = 2.0 * rate / (across * below), 2.0 * rate / (across * above)
    up_before = jnp.where(lane == 0, 0.0, pltpu.roll(up, 1, 1))
    low_after = jnp.where(lane == 127, 0.0, pltpu.roll(low, 127, 1))
    one = jnp.ones(shape, jnp.float32)
    t = prefix((1.0 + low, up_before, one, up_before), lane, False)
    tau = prefix((1.0 + up, low_after, one, low_after), lane, True)
    r = jnp.where(lane == 0, 0.0, low / (low + tau))
    s = jnp.where(lane == 127, 0.0, up / (up + t))
    g = 1.0 / (t + tau - 1.0)
    rs = jnp.where(row < 4, r, s)
    gc = jnp.where(row < 4, g, time_step / across)
    four = rs * pltpu.roll(rs, 127, 1)
    four = four * pltpu.roll(four, 126, 1)
    scan_ref[0:8, :] = four * pltpu.roll(four, 124, 1)
    scan_ref[8:16, :] = four
    turn = lax.rem(129 - 4 * chip_index(), 128)
    own_ref[0:8, :] = pltpu.roll(rs, turn, 1)
    own_ref[8:16, :] = pltpu.roll(gc, turn, 1)
    own_ref[16:24, :] = pltpu.roll(four, turn, 1)


def pair_factors(cf_ref, c):
    lower = lax.axis_index("zh") == 0
    r0 = jnp.where(lower, cf_ref[16 + c, 2], cf_ref[16 + c, 126])
    r1 = jnp.where(lower, cf_ref[16 + c, 6], cf_ref[16 + c, 2])
    s0 = jnp.where(lower, cf_ref[20 + c, 0], cf_ref[20 + c, 124])
    s1 = jnp.where(lower, cf_ref[20 + c, 4], cf_ref[20 + c, 0])
    return lower, r0, r1, s0, s1


def piece(half, block, down):
    return 8 * down + 4 * half + block // 2


def ends_kernel(own_ref, other_ref, out_ref):
    first = lax.axis_index("core") == 0
    for line in range(8):
        c, k = line // 2, line % 2
        for at, ref in ((line, own_ref), (8 + line, other_ref)):
            out_ref[at : at + 1, :] = jnp.where(first, ref[c, k, 0:1, :], ref[c, k, 31:32, :])


def local_kernel(own_ref, other_ref, halo_ref, cf_ref, dif_ref, part_ref, *send_refs):
    core = lax.axis_index("core")
    first = core == 0
    sub = lax.broadcasted_iota(jnp.int32, (8, 1024), 0)
    rate = time_step / (2.0 * cell_width)

    def tile(c, level, rows):
        return jnp.where(
            core == level // 2, own_ref[c, level % 2, rows, :], other_ref[c, level % 2, rows, :]
        )

    def far(c, level):
        line = 2 * c + level % 2
        return jnp.where(
            core == level // 2, halo_ref[8 + line : 9 + line, :], halo_ref[line : line + 1, :]
        )

    for half in range(2):
        rows = pl.ds(pl.multiple_of(core * 16 + 8 * half, 8), 8)
        here = slice(8 * half, 8 * half + 8)
        u = [tile(0, level, rows) * rate for level in range(4)]
        v = [tile(1, level, rows) * rate for level in range(4)]
        w = [tile(2, level, rows) for level in range(4)]
        wc = [w[level] * cf_ref[12, level + 1] for level in range(4)]
        for c in range(4):
            r = [cf_ref[c, j] for j in range(6)]
            s = [cf_ref[4 + c, j] for j in range(6)]
            g = [cf_ref[8 + c, j] for j in range(6)]
            spread = dif_ref[c] * (time_step / cell_width**2)
            q = w if c == 2 else [tile(c, level, rows) for level in range(4)]
            gs = []
            for level in range(4):
                centre = q[level]
                left, right = pltpu.roll(centre, 1, 1), pltpu.roll(centre, 1023, 1)
                if half == 0:
                    top = jnp.where(first, far(c, level), tile(c, level, slice(15, 16)))
                    bottom = tile(c, level, pl.ds(pl.multiple_of(core * 16 + 8, 8), 8))[:1]
                else:
                    top = tile(c, level, pl.ds(pl.multiple_of(core * 16, 8), 8))[7:]
                    bottom = jnp.where(first, tile(c, level, slice(16, 17)), far(c, level))
                front = jnp.where(sub == 0, top, pltpu.roll(centre, 1, 0))
                back = jnp.where(sub == 7, bottom, pltpu.roll(centre, 7, 0))
                total = centre + spread * ((left + right) + (front + back) - 4.0 * centre)
                total = total - u[level] * (right - left) - v[level] * (back - front)
                if level == 0:
                    total = total - wc[0] * q[1]
                elif level == 3:
                    total = total + wc[3] * q[2]
                else:
                    total = total - wc[level] * (q[level + 1] - q[level - 1])
                if c == 2:
                    total = total + (time_step * buoyancy) * tile(3, level, rows)
                elif c == 3:
                    total = total + time_step * w[level]
                gs.append(g[level + 1] * total)
            a = [gs[0]]
            for level in range(1, 4):
                a.append(r[level + 1] * a[-1] + gs[level])
            p = r[5] * a[3]
            part_ref[c, 3, here, :] = a[3]
            b = s[3] * gs[3]
            part_ref[c, 2, here, :] = a[2] + b
            for level in (1, 0):
                b = s[level + 1] * (b + gs[level + 1])
                part_ref[c, level, here, :] = a[level] + b
            b = s[0] * (b + gs[0])
            for block in range(8):
                lanes = slice(128 * block, 128 * block + 128)
                send_refs[c // 2][piece(half, block, 0), c % 2, block % 2] = p[:, lanes]
                send_refs[c // 2][piece(half, block, 1), c % 2, block % 2] = b[:, lanes]


def weights(cf_ref, c):
    r = [cf_ref[c, j] for j in range(6)]
    s = [cf_ref[4 + c, j] for j in range(6)]
    rise = [1.0, r[2], r[2] * r[3], r[2] * r[3] * r[4]]
    return rise, [s[1] * s[2] * s[3], s[2] * s[3], s[3], 1.0]


def edges_kernel(
    own_ref, other_ref, far_ref, near_ref, raw01_ref, raw23_ref, old_ref, cf_ref,
    sum01_ref, sum23_ref, part_ref,
):
    core = lax.axis_index("core")
    first = core == 0
    for half in range(2):
        rows = pl.ds(pl.multiple_of(core * 16 + 8 * half, 8), 8)
        far, near = far_ref[rows, :], near_ref[rows, :]
        w_low = jnp.where(first, far, near) * -cf_ref[12, 0]
        w_high = jnp.where(first, near, far) * cf_ref[12, 5]
        for c in range(4):
            raw_ref, sum_ref = ((raw01_ref, sum01_ref), (raw23_ref, sum23_ref))[c // 2]
            r = [cf_ref[c, j] for j in range(6)]
            s = [cf_ref[4 + c, j] for j in range(6)]
            lowest = jnp.where(first, own_ref[c, 0, rows, :], other_ref[c, 0, rows, :])
            highest = jnp.where(first, other_ref[c, 1, rows, :], own_ref[c, 1, rows, :])
            low, high = cf_ref[8 + c, 0] * (w_low * lowest), cf_ref[8 + c, 5] * (w_high * highest)
            from_low, from_high = r[1] * low, s[4] * high
            p = (r[2] * r[3] * r[4] * r[5]) * from_low + high
            q = (s[0] * s[1] * s[2] * s[3]) * from_high + low
            for block in range(8):
                lanes = slice(128 * block, 128 * block + 128)
                up = piece(half, block, 0), c % 2, block % 2
                down = piece(half, block, 1), c % 2, block % 2
                sum_ref[up] = raw_ref[up] + p[:, lanes]
                sum_ref[down] = raw_ref[down] + q[:, lanes]
            rise, fall = weights(cf_ref, c)
            here = slice(8 * half, 8 * half + 8)
            for level in range(4):
                part_ref[c, level, here, :] = old_ref[c, level, here, :] + (
                    rise[level] * from_low + fall[level] * from_high
                )


def pair_kernel(own_ref, partner_ref, cf_ref, out_ref):
    for c in range(2):
        lower, _, r1, s0, _ = pair_factors(cf_ref, c)
        own_p, partner_p = jnp.where(lower, r1, 1.0), jnp.where(lower, 1.0, r1)
        own_q, partner_q = jnp.where(lower, 1.0, s0), jnp.where(lower, s0, 1.0)
        out_ref[0:8, c] = own_p * own_ref[0:8, c] + partner_p * partner_ref[0:8, c]
        out_ref[8:16, c] = own_q * own_ref[8:16, c] + partner_q * partner_ref[8:16, c]


def scan_kernel(base, in_ref, cf_ref, out_ref):
    upward = lax.axis_index("y") < 2
    lower = lax.axis_index("zh") == 0

    def scaled(pair, c, at, by):
        value = in_ref[pair, c]
        return value if base == 0 else jnp.where(by, cf_ref[8 + at, (8 * pair + 5 if at < 4 else 8 * pair + 127) % 128], 1.0) * value

    @pl.when(upward)
    def _():
        for c in range(2):
            carry = jnp.zeros((2, 8, 128), jnp.float32)
            for pair in range(16):
                out_ref[pair, c] = carry
                carry = cf_ref[base + c, 8 * pair + 1] * carry + scaled(pair, c, base + c, lower)

    @pl.when(jnp.logical_not(upward))
    def _():
        for c in range(2):
            carry = jnp.zeros((2, 8, 128), jnp.float32)
            for pair in range(15, -1, -1):
                out_ref[pair, c] = carry
                at = 4 + base + c
                kept = cf_ref[at, (8 * pair + 127) % 128] * carry
                carry = kept + scaled(pair, c, at, jnp.logical_not(lower))


def crossing_kernel(own_ref, carry_ref, cf_ref, out_ref):
    for c in range(2):
        lower, r0, _, _, s1 = pair_factors(cf_ref, 2 + c)
        up, down = carry_ref[0:8, c], carry_ref[8:16, c]
        out_ref[0:8, c] = jnp.where(lower, r0 * up + own_ref[0:8, c], up)
        out_ref[8:16, c] = jnp.where(lower, down, s1 * down + own_ref[8:16, c])


def finish_kernel(
    kept, part_ref, carry01_ref, partner01_ref, carry23_ref, partner23_ref, cf_ref, out_ref
):
    core = lax.axis_index("core")
    upper = (core == 1) if kept else (core == 0)
    base = 2 * core if kept else 2 - 2 * core
    for c in range(4):
        carry_ref, partner_ref = (
            (carry01_ref, partner01_ref),
            (carry23_ref, partner23_ref),
        )[c // 2]
        lower, r0, _, _, s1 = pair_factors(cf_ref, c)
        by_p, by_q = jnp.where(lower, 1.0, r0), jnp.where(lower, s1, 1.0)
        rise, fall = weights(cf_ref, c)
        rises = [jnp.where(upper, rise[2 + k], rise[k]) for k in range(2)]
        falls = [jnp.where(upper, fall[2 + k], fall[k]) for k in range(2)]
        for half in range(2):
            here = slice(8 * half, 8 * half + 8)
            rows = pl.ds(pl.multiple_of(core * 16 + 8 * half, 8), 8) if kept else here
            for block in range(8):
                lanes = slice(128 * block, 128 * block + 128)
                up = piece(half, block, 0), c % 2, block % 2
                down = piece(half, block, 1), c % 2, block % 2
                p = by_p * carry_ref[up]
                q = by_q * carry_ref[down]
                if c < 2:
                    p = p + jnp.where(lower, 0.0, partner_ref[up])
                    q = q + jnp.where(lower, partner_ref[down], 0.0)
                else:
                    p, q = p + partner_ref[up], q + partner_ref[down]
                for k in range(2):
                    own = part_ref[c, base + k, here, lanes]
                    out_ref[c, k, rows, lanes] = own + rises[k] * p + falls[k] * q


def shards(flow_state, spacing, diffusivity):
    core = lax.axis_index("core")
    f32 = jnp.float32

    def route(value, axes, sizes, to):
        pairs = []
        for source in range(int(np.prod(sizes))):
            target = to(*(int(i) for i in np.unravel_index(source, sizes)))
            if target is not None:
                pairs.append((source, target))
        return lax.ppermute(value, axes, pairs)

    def across_cores(value):
        return lax.ppermute(value, "core", [(0, 1), (1, 0)])

    def within(chip, k):
        return 2 * chip + k if 0 <= chip < 32 else None

    def to_chip(chip, k):
        return within(chip + 1 if k else chip - 1, 1 - k)

    def to_col(k, z):
        return (1 - k) * 8 + (z + (1 if k else -1)) % 8

    other = across_cores(flow_state)
    edge = lax.dynamic_slice(flow_state, (2, core, 0, 0), (1, 1, 32, 1024)).reshape(32, 1024)
    w_far = route(edge, ROW, (32, 2), to_chip)
    ends = pl.pallas_call(
        ends_kernel,
        out_shape=jax.ShapeDtypeStruct((16, 1024), f32),
        in_specs=[whole()] * 2,
        out_specs=whole(),
        compiler_params=params(),
        name="row_ends",
    )(flow_state, other)
    halo = route(ends, ("core", "zl"), (2, 8), to_col)

    own_cf, scan_cf = pl.pallas_call(
        coefficients_kernel,
        out_shape=(jax.ShapeDtypeStruct((24, 128), f32), jax.ShapeDtypeStruct((16, 128), f32)),
        in_specs=[whole(), whole(pltpu.SMEM)],
        out_specs=(whole(), whole()),
        compiler_params=params(),
        name="coefficients",
    )(spacing.reshape(1, 128), diffusivity)

    def call(kernel, name, outs, *args, **more):
        smem = {id(own_cf), id(scan_cf), id(diffusivity)}
        return pl.pallas_call(
            kernel,
            out_shape=outs,
            in_specs=[whole(pltpu.SMEM if id(a) in smem else pltpu.VMEM) for a in args],
            out_specs=jax.tree.map(lambda _: whole(), outs),
            compiler_params=params(),
            name=name,
            **more,
        )(*args)

    def in_plane(value):
        return lax.all_to_all(value, ("y", "x"), split_axis=0, concat_axis=0, tiled=True)

    def to_partner(value):
        return lax.ppermute(value, "zh", [(0, 1), (1, 0)])

    def sent_back(value, base):
        kernel = functools.partial(scan_kernel, base)
        return in_plane(call(kernel, "scan_pairs", pieces, value, scan_cf))

    def in_loop(step, value):
        once = lax.optimization_barrier(jnp.int32(1))
        return lax.while_loop(
            lambda state: state[0] > 0, lambda state: (jnp.int32(0), step(state[1])), (once, value)
        )[1]

    def array(*shape):
        return jax.ShapeDtypeStruct(shape, f32)

    pieces = array(16, 2, 2, 8, 128)
    halo, w_far, own_cf, scan_cf = lax.optimization_barrier((halo, w_far, own_cf, scan_cf))
    w_near = across_cores(w_far)
    part, raw01, raw23 = call(
        local_kernel,
        "local_step",
        (array(4, 4, 16, 1024), pieces, pieces),
        flow_state, other, halo, own_cf, diffusivity,
    )
    sum01, sum23, part = call(
        edges_kernel,
        "edge_products",
        (pieces, pieces, array(4, 4, 16, 1024)),
        flow_state, other, w_far, w_near, raw01, raw23, part, own_cf,
        input_output_aliases={4: 0, 5: 1, 6: 2},
    )

    partner01 = to_partner(sum01)
    carry23 = in_loop(lambda value: sent_back(value, 2), in_plane(sum23))
    leaving23 = call(crossing_kernel, "crossing", pieces, sum23, carry23, own_cf)
    partner23 = to_partner(leaving23)

    def scan_pairs01(value):
        moments = call(pair_kernel, "pair_moments", pieces, value, partner01, own_cf)
        return sent_back(in_plane(moments), 0)

    sum01, _ = lax.optimization_barrier((sum01, leaving23))
    carry01 = in_loop(scan_pairs01, sum01)
    ready = part, carry01, partner01, carry23, partner23, own_cf
    leaving = call(
        functools.partial(finish_kernel, False), "finish_other", array(4, 2, 16, 1024), *ready
    )
    back = across_cores(leaving)
    kept = call(functools.partial(finish_kernel, True), "finish_own", array(4, 2, 32, 1024), *ready)
    return lax.dynamic_update_slice_in_dim(kept, back, 16 * (1 - core), 2)


def solution(mesh):
    fine = Mesh(mesh.devices.reshape(4, 4, 2, 2, 8), AXES)
    field = P(None, ROW, "zl", None)
    return jax.shard_map(
        shards, mesh=fine, in_specs=(field, P(), P()), out_specs=field, check_vma=False
    )
```

```python
import functools

import jax
import jax.numpy as jnp
import numpy as np
from jax import lax
from jax.experimental import pallas as pl
from jax.experimental.pallas import tpu as pltpu
from jax.sharding import Mesh
from jax.sharding import PartitionSpec as P

time_step = 0.02
cell_width = 0.1
buoyancy = 1.0

AXES = ("y", "x", "zh", "core", "zl")
ROW = AXES[:4]
PLANE = AXES[:3]
LIMIT = 12 * 2**20


def whole(space=pltpu.VMEM):
    return pl.BlockSpec(memory_space=space)


def params():
    return pltpu.CompilerParams(vmem_limit_bytes=LIMIT)


def prefix(matrix, lane, backward):
    a, b, c, d = matrix
    step = 1
    while step < 128:
        by = 128 - step if backward else step
        edge = lane >= 128 - step if backward else lane < step
        pa, pb, pc, pd = (pltpu.roll(m, by, 1) for m in (a, b, c, d))
        pa, pb = jnp.where(edge, 1.0, pa), jnp.where(edge, 0.0, pb)
        pc, pd = jnp.where(edge, 0.0, pc), jnp.where(edge, 1.0, pd)
        a, b, c, d = a * pa + b * pc, a * pb + b * pd, c * pa + d * pc, c * pb + d * pd
        scale = 1.0 / (a + b + c + d)
        a, b, c, d = a * scale, b * scale, c * scale, d * scale
        step *= 2
    return (a + b) / (c + d)


def chip_index():
    return (lax.axis_index("y") * 4 + lax.axis_index("x")) * 2 + lax.axis_index("zh")


def coefficients_kernel(spacing_ref, diffusivity_ref, own_ref, scan_ref):
    shape = (8, 128)
    lane = lax.broadcasted_iota(jnp.int32, shape, 1)
    row = lax.broadcasted_iota(jnp.int32, shape, 0)
    below = jnp.broadcast_to(spacing_ref[...], shape)
    above = jnp.where(lane == 127, below, pltpu.roll(below, 127, 1))
    across = below + above
    rate = jnp.full(shape, diffusivity_ref[3], jnp.float32)
    for component in range(3):
        rate = jnp.where(row % 4 == component, diffusivity_ref[component], rate)
    rate = time_step * rate
    low, up = 2.0 * rate / (across * below), 2.0 * rate / (across * above)
    up_before = jnp.where(lane == 0, 0.0, pltpu.roll(up, 1, 1))
    low_after = jnp.where(lane == 127, 0.0, pltpu.roll(low, 127, 1))
    one = jnp.ones(shape, jnp.float32)
    t = prefix((1.0 + low, up_before, one, up_before), lane, False)
    tau = prefix((1.0 + up, low_after, one, low_after), lane, True)
    r = jnp.where(lane == 0, 0.0, low / (low + tau))
    s = jnp.where(lane == 127, 0.0, up / (up + t))
    g = 1.0 / (t + tau - 1.0)
    rs = jnp.where(row < 4, r, s)
    gc = jnp.where(row < 4, g, time_step / across)
    four = rs * pltpu.roll(rs, 127, 1)
    four = four * pltpu.roll(four, 126, 1)
    scan_ref[0:8, :] = four * pltpu.roll(four, 124, 1)
    scan_ref[8:16, :] = four
    turn = lax.rem(129 - 4 * chip_index(), 128)
    own_ref[0:8, :] = pltpu.roll(rs, turn, 1)
    own_ref[8:16, :] = pltpu.roll(gc, turn, 1)
    own_ref[16:24, :] = pltpu.roll(four, turn, 1)


def pair_factors(cf_ref, c):
    lower = lax.axis_index("zh") == 0
    r0 = jnp.where(lower, cf_ref[16 + c, 2], cf_ref[16 + c, 126])
    r1 = jnp.where(lower, cf_ref[16 + c, 6], cf_ref[16 + c, 2])
    s0 = jnp.where(lower, cf_ref[20 + c, 0], cf_ref[20 + c, 124])
    s1 = jnp.where(lower, cf_ref[20 + c, 4], cf_ref[20 + c, 0])
    return lower, r0, r1, s0, s1


def piece(half, block, down):
    return 8 * down + 4 * half + block // 2


def ends_kernel(own_ref, other_ref, out_ref, held, arrived):
    core = lax.axis_index("core")
    first = core == 0
    rows = pl.ds(pl.multiple_of(24 * core, 8), 8)
    fetch = pltpu.make_async_copy(own_ref.at[:, :, rows, :], held, arrived)
    fetch.start()
    for c in range(4):
        for k in range(2):
            row = jnp.where(first, other_ref[c, k, 0:1, :], other_ref[c, k, 31:32, :])
            out_ref[8 + 2 * c + k : 9 + 2 * c + k, :] = row
    fetch.wait()
    for c in range(4):
        for k in range(2):
            row = jnp.where(first, held[c, k, 0:1, :], held[c, k, 7:8, :])
            out_ref[2 * c + k : 2 * c + k + 1, :] = row


def local_kernel(own_ref, other_ref, halo_ref, cf_ref, dif_ref, part_ref, *send_refs):
    core = lax.axis_index("core")
    first = core == 0
    sub = lax.broadcasted_iota(jnp.int32, (8, 1024), 0)
    rate = time_step / (2.0 * cell_width)

    def tile(c, level, rows):
        return jnp.where(
            core == level // 2, own_ref[c, level % 2, rows, :], other_ref[c, level % 2, rows, :]
        )

    def far(c, level):
        line = 2 * c + level % 2
        return jnp.where(
            core == level // 2, halo_ref[8 + line : 9 + line, :], halo_ref[line : line + 1, :]
        )

    for half in range(2):
        rows = pl.ds(pl.multiple_of(core * 16 + 8 * half, 8), 8)
        here = slice(8 * half, 8 * half + 8)
        u = [tile(0, level, rows) * rate for level in range(4)]
        v = [tile(1, level, rows) * rate for level in range(4)]
        w = [tile(2, level, rows) for level in range(4)]
        wc = [w[level] * cf_ref[12, level + 1] for level in range(4)]
        for c in range(4):
            r = [cf_ref[c, j] for j in range(6)]
            s = [cf_ref[4 + c, j] for j in range(6)]
            g = [cf_ref[8 + c, j] for j in range(6)]
            spread = dif_ref[c] * (time_step / cell_width**2)
            q = w if c == 2 else [tile(c, level, rows) for level in range(4)]
            gs = []
            for level in range(4):
                centre = q[level]
                left, right = pltpu.roll(centre, 1, 1), pltpu.roll(centre, 1023, 1)
                if half == 0:
                    top = jnp.where(first, far(c, level), tile(c, level, slice(15, 16)))
                    bottom = tile(c, level, pl.ds(pl.multiple_of(core * 16 + 8, 8), 8))[:1]
                else:
                    top = tile(c, level, pl.ds(pl.multiple_of(core * 16, 8), 8))[7:]
                    bottom = jnp.where(first, tile(c, level, slice(16, 17)), far(c, level))
                front = jnp.where(sub == 0, top, pltpu.roll(centre, 1, 0))
                back = jnp.where(sub == 7, bottom, pltpu.roll(centre, 7, 0))
                total = centre + spread * ((left + right) + (front + back) - 4.0 * centre)
                total = total - u[level] * (right - left) - v[level] * (back - front)
                if level == 0:
                    total = total - wc[0] * q[1]
                elif level == 3:
                    total = total + wc[3] * q[2]
                else:
                    total = total - wc[level] * (q[level + 1] - q[level - 1])
                if c == 2:
                    total = total + (time_step * buoyancy) * tile(3, level, rows)
                elif c == 3:
                    total = total + time_step * w[level]
                gs.append(g[level + 1] * total)
            a = [gs[0]]
            for level in range(1, 4):
                a.append(r[level + 1] * a[-1] + gs[level])
            p = r[5] * a[3]
            part_ref[c, 3, here, :] = a[3]
            b = s[3] * gs[3]
            part_ref[c, 2, here, :] = a[2] + b
            for level in (1, 0):
                b = s[level + 1] * (b + gs[level + 1])
                part_ref[c, level, here, :] = a[level] + b
            b = s[0] * (b + gs[0])
            for block in range(8):
                lanes = slice(128 * block, 128 * block + 128)
                send_refs[c // 2][piece(half, block, 0), c % 2, block % 2] = p[:, lanes]
                send_refs[c // 2][piece(half, block, 1), c % 2, block % 2] = b[:, lanes]


def weights(cf_ref, c):
    r = [cf_ref[c, j] for j in range(6)]
    s = [cf_ref[4 + c, j] for j in range(6)]
    rise = [1.0, r[2], r[2] * r[3], r[2] * r[3] * r[4]]
    return rise, [s[1] * s[2] * s[3], s[2] * s[3], s[3], 1.0]


def edges_kernel(
    own_ref, other_ref, far_ref, near_ref, raw01_ref, raw23_ref, old_ref, cf_ref,
    sum01_ref, sum23_ref, part_ref,
):
    core = lax.axis_index("core")
    first = core == 0
    for half in range(2):
        rows = pl.ds(pl.multiple_of(core * 16 + 8 * half, 8), 8)
        far, near = far_ref[rows, :], near_ref[rows, :]
        w_low = jnp.where(first, far, near) * -cf_ref[12, 0]
        w_high = jnp.where(first, near, far) * cf_ref[12, 5]
        for c in range(4):
            raw_ref, sum_ref = ((raw01_ref, sum01_ref), (raw23_ref, sum23_ref))[c // 2]
            r = [cf_ref[c, j] for j in range(6)]
            s = [cf_ref[4 + c, j] for j in range(6)]
            lowest = jnp.where(first, own_ref[c, 0, rows, :], other_ref[c, 0, rows, :])
            highest = jnp.where(first, other_ref[c, 1, rows, :], own_ref[c, 1, rows, :])
            low, high = cf_ref[8 + c, 0] * (w_low * lowest), cf_ref[8 + c, 5] * (w_high * highest)
            from_low, from_high = r[1] * low, s[4] * high
            p = (r[2] * r[3] * r[4] * r[5]) * from_low + high
            q = (s[0] * s[1] * s[2] * s[3]) * from_high + low
            for block in range(8):
                lanes = slice(128 * block, 128 * block + 128)
                up = piece(half, block, 0), c % 2, block % 2
                down = piece(half, block, 1), c % 2, block % 2
                sum_ref[up] = raw_ref[up] + p[:, lanes]
                sum_ref[down] = raw_ref[down] + q[:, lanes]
            rise, fall = weights(cf_ref, c)
            here = slice(8 * half, 8 * half + 8)
            for level in range(4):
                part_ref[c, level, here, :] = old_ref[c, level, here, :] + (
                    rise[level] * from_low + fall[level] * from_high
                )


def pair_kernel(own_ref, partner_ref, cf_ref, out_ref):
    for c in range(2):
        lower, _, r1, s0, _ = pair_factors(cf_ref, c)
        own_p, partner_p = jnp.where(lower, r1, 1.0), jnp.where(lower, 1.0, r1)
        own_q, partner_q = jnp.where(lower, 1.0, s0), jnp.where(lower, s0, 1.0)
        out_ref[0:8, c] = own_p * own_ref[0:8, c] + partner_p * partner_ref[0:8, c]
        out_ref[8:16, c] = own_q * own_ref[8:16, c] + partner_q * partner_ref[8:16, c]


def scan_kernel(base, in_ref, cf_ref, out_ref):
    upward = lax.axis_index("y") < 2
    lower = lax.axis_index("zh") == 0

    def scaled(pair, c, at, by):
        value = in_ref[pair, c]
        return value if base == 0 else jnp.where(by, cf_ref[8 + at, (8 * pair + 5 if at < 4 else 8 * pair + 127) % 128], 1.0) * value

    @pl.when(upward)
    def _():
        for c in range(2):
            carry = jnp.zeros((2, 8, 128), jnp.float32)
            for pair in range(16):
                out_ref[pair, c] = carry
                carry = cf_ref[base + c, 8 * pair + 1] * carry + scaled(pair, c, base + c, lower)

    @pl.when(jnp.logical_not(upward))
    def _():
        for c in range(2):
            carry = jnp.zeros((2, 8, 128), jnp.float32)
            for pair in range(15, -1, -1):
                out_ref[pair, c] = carry
                at = 4 + base + c
                kept = cf_ref[at, (8 * pair + 127) % 128] * carry
                carry = kept + scaled(pair, c, at, jnp.logical_not(lower))


def crossing_kernel(own_ref, carry_ref, cf_ref, out_ref):
    for c in range(2):
        lower, r0, _, _, s1 = pair_factors(cf_ref, 2 + c)
        up, down = carry_ref[0:8, c], carry_ref[8:16, c]
        out_ref[0:8, c] = jnp.where(lower, r0 * up + own_ref[0:8, c], up)
        out_ref[8:16, c] = jnp.where(lower, down, s1 * down + own_ref[8:16, c])


def finish_kernel(
    kept, part_ref, carry01_ref, partner01_ref, carry23_ref, partner23_ref, cf_ref, out_ref
):
    core = lax.axis_index("core")
    upper = (core == 1) if kept else (core == 0)
    base = 2 * core if kept else 2 - 2 * core
    for c in range(4):
        carry_ref, partner_ref = (
            (carry01_ref, partner01_ref),
            (carry23_ref, partner23_ref),
        )[c // 2]
        lower, r0, _, _, s1 = pair_factors(cf_ref, c)
        by_p, by_q = jnp.where(lower, 1.0, r0), jnp.where(lower, s1, 1.0)
        rise, fall = weights(cf_ref, c)
        rises = [jnp.where(upper, rise[2 + k], rise[k]) for k in range(2)]
        falls = [jnp.where(upper, fall[2 + k], fall[k]) for k in range(2)]
        for half in range(2):
            here = slice(8 * half, 8 * half + 8)
            rows = pl.ds(pl.multiple_of(core * 16 + 8 * half, 8), 8) if kept else here
            for block in range(8):
                lanes = slice(128 * block, 128 * block + 128)
                up = piece(half, block, 0), c % 2, block % 2
                down = piece(half, block, 1), c % 2, block % 2
                p = by_p * carry_ref[up]
                q = by_q * carry_ref[down]
                if c < 2:
                    p = p + jnp.where(lower, 0.0, partner_ref[up])
                    q = q + jnp.where(lower, partner_ref[down], 0.0)
                else:
                    p, q = p + partner_ref[up], q + partner_ref[down]
                for k in range(2):
                    own = part_ref[c, base + k, here, lanes]
                    out_ref[c, k, rows, lanes] = own + rises[k] * p + falls[k] * q


def shards(flow_state, spacing, diffusivity):
    core = lax.axis_index("core")
    f32 = jnp.float32

    def route(value, axes, sizes, to):
        pairs = []
        for source in range(int(np.prod(sizes))):
            target = to(*(int(i) for i in np.unravel_index(source, sizes)))
            if target is not None:
                pairs.append((source, target))
        return lax.ppermute(value, axes, pairs)

    def across_cores(value):
        return lax.ppermute(value, "core", [(0, 1), (1, 0)])

    def within(chip, k):
        return 2 * chip + k if 0 <= chip < 32 else None

    def to_chip(chip, k):
        return within(chip + 1 if k else chip - 1, 1 - k)

    def to_col(k, z):
        return (1 - k) * 8 + (z + (1 if k else -1)) % 8

    other = across_cores(flow_state)
    edge = lax.dynamic_slice(flow_state, (2, core, 0, 0), (1, 1, 32, 1024)).reshape(32, 1024)
    w_far = route(edge, ROW, (32, 2), to_chip)
    ends = pl.pallas_call(
        ends_kernel,
        out_shape=jax.ShapeDtypeStruct((16, 1024), f32),
        in_specs=[whole(pltpu.HBM), whole()],
        out_specs=whole(),
        scratch_shapes=[pltpu.VMEM((4, 2, 8, 1024), f32), pltpu.SemaphoreType.DMA],
        compiler_params=params(),
        name="row_ends",
    )(flow_state, other)
    halo = route(ends, ("core", "zl"), (2, 8), to_col)

    own_cf, scan_cf = pl.pallas_call(
        coefficients_kernel,
        out_shape=(jax.ShapeDtypeStruct((24, 128), f32), jax.ShapeDtypeStruct((16, 128), f32)),
        in_specs=[whole(), whole(pltpu.SMEM)],
        out_specs=(whole(), whole()),
        compiler_params=params(),
        name="coefficients",
    )(spacing.reshape(1, 128), diffusivity)

    def call(kernel, name, outs, *args, **more):
        smem = {id(own_cf), id(scan_cf), id(diffusivity)}
        return pl.pallas_call(
            kernel,
            out_shape=outs,
            in_specs=[whole(pltpu.SMEM if id(a) in smem else pltpu.VMEM) for a in args],
            out_specs=jax.tree.map(lambda _: whole(), outs),
            compiler_params=params(),
            name=name,
            **more,
        )(*args)

    def in_plane(value):
        return lax.all_to_all(value, ("y", "x"), split_axis=0, concat_axis=0, tiled=True)

    def to_partner(value):
        return lax.ppermute(value, "zh", [(0, 1), (1, 0)])

    def sent_back(value, base):
        kernel = functools.partial(scan_kernel, base)
        return in_plane(call(kernel, "scan_pairs", pieces, value, scan_cf))

    def in_loop(step, value):
        def body(state):
            left, held = lax.optimization_barrier((state[0] - 1, state[1]))
            return left, step(held)

        once = lax.optimization_barrier(jnp.int32(1))
        return lax.while_loop(lambda state: state[0] > 0, body, (once, value))[1]

    def array(*shape):
        return jax.ShapeDtypeStruct(shape, f32)

    pieces = array(16, 2, 2, 8, 128)
    halo, w_far, own_cf, scan_cf = lax.optimization_barrier((halo, w_far, own_cf, scan_cf))
    w_near = across_cores(w_far)
    part, raw01, raw23 = call(
        local_kernel,
        "local_step",
        (array(4, 4, 16, 1024), pieces, pieces),
        flow_state, other, halo, own_cf, diffusivity,
    )
    sum01, sum23, part = call(
        edges_kernel,
        "edge_products",
        (pieces, pieces, array(4, 4, 16, 1024)),
        flow_state, other, w_far, w_near, raw01, raw23, part, own_cf,
        input_output_aliases={4: 0, 5: 1, 6: 2},
    )

    partner01 = to_partner(sum01)
    carry23 = in_loop(lambda value: sent_back(in_plane(value), 2), sum23)
    leaving23 = call(crossing_kernel, "crossing", pieces, sum23, carry23, own_cf)
    partner23 = to_partner(leaving23)

    def scan_pairs01(value):
        moments = call(pair_kernel, "pair_moments", pieces, value, partner01, own_cf)
        return sent_back(in_plane(moments), 0)

    sum01, _ = lax.optimization_barrier((sum01, leaving23))
    carry01 = in_loop(scan_pairs01, sum01)
    ready = part, carry01, partner01, carry23, partner23, own_cf
    leaving = call(
        functools.partial(finish_kernel, False), "finish_other", array(4, 2, 16, 1024), *ready
    )
    back = across_cores(leaving)
    kept = call(functools.partial(finish_kernel, True), "finish_own", array(4, 2, 32, 1024), *ready)
    return lax.dynamic_update_slice_in_dim(kept, back, 16 * (1 - core), 2)


def solution(mesh):
    fine = Mesh(mesh.devices.reshape(4, 4, 2, 2, 8), AXES)
    field = P(None, ROW, "zl", None)
    return jax.shard_map(
        shards, mesh=fine, in_specs=(field, P(), P()), out_specs=field, check_vma=False
    )
```

```python
import functools

import jax
import jax.numpy as jnp
import numpy as np
from jax import lax
from jax.experimental import pallas as pl
from jax.experimental.pallas import tpu as pltpu
from jax.sharding import Mesh
from jax.sharding import PartitionSpec as P

time_step = 0.02
cell_width = 0.1
buoyancy = 1.0

AXES = ("y", "x", "zh", "core", "zl")
ROW = AXES[:4]
PLANE = AXES[:3]
LIMIT = 12 * 2**20


def whole(space=pltpu.VMEM):
    return pl.BlockSpec(memory_space=space)


def params():
    return pltpu.CompilerParams(vmem_limit_bytes=LIMIT)


def prefix(matrix, lane, backward):
    a, b, c, d = matrix
    step = 1
    while step < 128:
        by = 128 - step if backward else step
        edge = lane >= 128 - step if backward else lane < step
        pa, pb, pc, pd = (pltpu.roll(m, by, 1) for m in (a, b, c, d))
        pa, pb = jnp.where(edge, 1.0, pa), jnp.where(edge, 0.0, pb)
        pc, pd = jnp.where(edge, 0.0, pc), jnp.where(edge, 1.0, pd)
        a, b, c, d = a * pa + b * pc, a * pb + b * pd, c * pa + d * pc, c * pb + d * pd
        scale = 1.0 / (a + b + c + d)
        a, b, c, d = a * scale, b * scale, c * scale, d * scale
        step *= 2
    return (a + b) / (c + d)


def chip_index():
    return (lax.axis_index("y") * 4 + lax.axis_index("x")) * 2 + lax.axis_index("zh")


def coefficients_kernel(spacing_ref, diffusivity_ref, own_ref, scan_ref):
    shape = (8, 128)
    lane = lax.broadcasted_iota(jnp.int32, shape, 1)
    row = lax.broadcasted_iota(jnp.int32, shape, 0)
    below = jnp.broadcast_to(spacing_ref[...], shape)
    above = jnp.where(lane == 127, below, pltpu.roll(below, 127, 1))
    across = below + above
    rate = jnp.full(shape, diffusivity_ref[3], jnp.float32)
    for component in range(3):
        rate = jnp.where(row % 4 == component, diffusivity_ref[component], rate)
    rate = time_step * rate
    low, up = 2.0 * rate / (across * below), 2.0 * rate / (across * above)
    up_before = jnp.where(lane == 0, 0.0, pltpu.roll(up, 1, 1))
    low_after = jnp.where(lane == 127, 0.0, pltpu.roll(low, 127, 1))
    one = jnp.ones(shape, jnp.float32)
    t = prefix((1.0 + low, up_before, one, up_before), lane, False)
    tau = prefix((1.0 + up, low_after, one, low_after), lane, True)
    r = jnp.where(lane == 0, 0.0, low / (low + tau))
    s = jnp.where(lane == 127, 0.0, up / (up + t))
    g = 1.0 / (t + tau - 1.0)
    rs = jnp.where(row < 4, r, s)
    gc = jnp.where(row < 4, g, time_step / across)
    four = rs * pltpu.roll(rs, 127, 1)
    four = four * pltpu.roll(four, 126, 1)
    scan_ref[0:8, :] = four * pltpu.roll(four, 124, 1)
    scan_ref[8:16, :] = four
    turn = lax.rem(129 - 4 * chip_index(), 128)
    own_ref[0:8, :] = pltpu.roll(rs, turn, 1)
    own_ref[8:16, :] = pltpu.roll(gc, turn, 1)
    own_ref[16:24, :] = pltpu.roll(four, turn, 1)


def entry(ref, row, lane):
    return ref[row : row + 1, lane : lane + 1]


def pair_factors(cf_ref, c):
    lower = lax.axis_index("zh") == 0
    r0 = jnp.where(lower, entry(cf_ref, 16 + c, 2), entry(cf_ref, 16 + c, 126))
    r1 = jnp.where(lower, entry(cf_ref, 16 + c, 6), entry(cf_ref, 16 + c, 2))
    s0 = jnp.where(lower, entry(cf_ref, 20 + c, 0), entry(cf_ref, 20 + c, 124))
    s1 = jnp.where(lower, entry(cf_ref, 20 + c, 4), entry(cf_ref, 20 + c, 0))
    return lower, r0, r1, s0, s1


def piece(half, block, down):
    return 8 * down + 4 * half + block // 2


def ends_kernel(own_ref, other_ref, out_ref, held, arrived):
    core = lax.axis_index("core")
    first = core == 0
    rows = pl.ds(pl.multiple_of(24 * core, 8), 8)
    fetch = pltpu.make_async_copy(own_ref.at[:, :, rows, :], held, arrived)
    fetch.start()
    for c in range(4):
        for k in range(2):
            row = jnp.where(first, other_ref[c, k, 0:1, :], other_ref[c, k, 31:32, :])
            out_ref[8 + 2 * c + k : 9 + 2 * c + k, :] = row
    fetch.wait()
    for c in range(4):
        for k in range(2):
            row = jnp.where(first, held[c, k, 0:1, :], held[c, k, 7:8, :])
            out_ref[2 * c + k : 2 * c + k + 1, :] = row


def local_kernel(own_ref, other_ref, halo_ref, cf_ref, dif_ref, part_ref, *send_refs):
    core = lax.axis_index("core")
    first = core == 0
    sub = lax.broadcasted_iota(jnp.int32, (8, 1024), 0)
    rate = time_step / (2.0 * cell_width)

    def tile(c, level, rows):
        return jnp.where(
            core == level // 2, own_ref[c, level % 2, rows, :], other_ref[c, level % 2, rows, :]
        )

    def far(c, level):
        line = 2 * c + level % 2
        return jnp.where(
            core == level // 2, halo_ref[8 + line : 9 + line, :], halo_ref[line : line + 1, :]
        )

    for half in range(2):
        rows = pl.ds(pl.multiple_of(core * 16 + 8 * half, 8), 8)
        here = slice(8 * half, 8 * half + 8)
        u = [tile(0, level, rows) * rate for level in range(4)]
        v = [tile(1, level, rows) * rate for level in range(4)]
        w = [tile(2, level, rows) for level in range(4)]
        wc = [w[level] * cf_ref[12, level + 1] for level in range(4)]
        for c in range(4):
            r = [cf_ref[c, j] for j in range(6)]
            s = [cf_ref[4 + c, j] for j in range(6)]
            g = [cf_ref[8 + c, j] for j in range(6)]
            spread = dif_ref[c] * (time_step / cell_width**2)
            q = w if c == 2 else [tile(c, level, rows) for level in range(4)]
            gs = []
            for level in range(4):
                centre = q[level]
                left, right = pltpu.roll(centre, 1, 1), pltpu.roll(centre, 1023, 1)
                if half == 0:
                    top = jnp.where(first, far(c, level), tile(c, level, slice(15, 16)))
                    bottom = tile(c, level, pl.ds(pl.multiple_of(core * 16 + 8, 8), 8))[:1]
                else:
                    top = tile(c, level, pl.ds(pl.multiple_of(core * 16, 8), 8))[7:]
                    bottom = jnp.where(first, tile(c, level, slice(16, 17)), far(c, level))
                front = jnp.where(sub == 0, top, pltpu.roll(centre, 1, 0))
                back = jnp.where(sub == 7, bottom, pltpu.roll(centre, 7, 0))
                total = centre + spread * ((left + right) + (front + back) - 4.0 * centre)
                total = total - u[level] * (right - left) - v[level] * (back - front)
                if level == 0:
                    total = total - wc[0] * q[1]
                elif level == 3:
                    total = total + wc[3] * q[2]
                else:
                    total = total - wc[level] * (q[level + 1] - q[level - 1])
                if c == 2:
                    total = total + (time_step * buoyancy) * tile(3, level, rows)
                elif c == 3:
                    total = total + time_step * w[level]
                gs.append(g[level + 1] * total)
            a = [gs[0]]
            for level in range(1, 4):
                a.append(r[level + 1] * a[-1] + gs[level])
            p = r[5] * a[3]
            part_ref[c, 3, here, :] = a[3]
            b = s[3] * gs[3]
            part_ref[c, 2, here, :] = a[2] + b
            for level in (1, 0):
                b = s[level + 1] * (b + gs[level + 1])
                part_ref[c, level, here, :] = a[level] + b
            b = s[0] * (b + gs[0])
            for block in range(8):
                lanes = slice(128 * block, 128 * block + 128)
                send_refs[c // 2][piece(half, block, 0), c % 2, block % 2] = p[:, lanes]
                send_refs[c // 2][piece(half, block, 1), c % 2, block % 2] = b[:, lanes]


def weights(cf_ref, c):
    r = [entry(cf_ref, c, j) for j in range(6)]
    s = [entry(cf_ref, 4 + c, j) for j in range(6)]
    rise = [1.0, r[2], r[2] * r[3], r[2] * r[3] * r[4]]
    return rise, [s[1] * s[2] * s[3], s[2] * s[3], s[3], 1.0]


def edges_kernel(
    own_ref, other_ref, far_ref, near_ref, raw01_ref, raw23_ref, old_ref, cf_ref,
    sum01_ref, sum23_ref, part_ref,
):
    core = lax.axis_index("core")
    first = core == 0
    for half in range(2):
        rows = pl.ds(pl.multiple_of(core * 16 + 8 * half, 8), 8)
        far, near = far_ref[rows, :], near_ref[rows, :]
        w_low = jnp.where(first, far, near) * -entry(cf_ref, 12, 0)
        w_high = jnp.where(first, near, far) * entry(cf_ref, 12, 5)
        for c in range(4):
            raw_ref, sum_ref = ((raw01_ref, sum01_ref), (raw23_ref, sum23_ref))[c // 2]
            r = [entry(cf_ref, c, j) for j in range(6)]
            s = [entry(cf_ref, 4 + c, j) for j in range(6)]
            lowest = jnp.where(first, own_ref[c, 0, rows, :], other_ref[c, 0, rows, :])
            highest = jnp.where(first, other_ref[c, 1, rows, :], own_ref[c, 1, rows, :])
            low, high = entry(cf_ref, 8 + c, 0) * (w_low * lowest), entry(cf_ref, 8 + c, 5) * (w_high * highest)
            from_low, from_high = r[1] * low, s[4] * high
            p = (r[2] * r[3] * r[4] * r[5]) * from_low + high
            q = (s[0] * s[1] * s[2] * s[3]) * from_high + low
            for block in range(8):
                lanes = slice(128 * block, 128 * block + 128)
                up = piece(half, block, 0), c % 2, block % 2
                down = piece(half, block, 1), c % 2, block % 2
                sum_ref[up] = raw_ref[up] + p[:, lanes]
                sum_ref[down] = raw_ref[down] + q[:, lanes]
            rise, fall = weights(cf_ref, c)
            here = slice(8 * half, 8 * half + 8)
            for level in range(4):
                part_ref[c, level, here, :] = old_ref[c, level, here, :] + (
                    rise[level] * from_low + fall[level] * from_high
                )


def pair_kernel(own_ref, partner_ref, cf_ref, out_ref):
    for c in range(2):
        lower, _, r1, s0, _ = pair_factors(cf_ref, c)
        own_p, partner_p = jnp.where(lower, r1, 1.0), jnp.where(lower, 1.0, r1)
        own_q, partner_q = jnp.where(lower, 1.0, s0), jnp.where(lower, s0, 1.0)
        out_ref[0:8, c] = own_p * own_ref[0:8, c] + partner_p * partner_ref[0:8, c]
        out_ref[8:16, c] = own_q * own_ref[8:16, c] + partner_q * partner_ref[8:16, c]


def scan_kernel(base, in_ref, cf_ref, out_ref):
    upward = lax.axis_index("y") < 2
    lower = lax.axis_index("zh") == 0

    def scaled(pair, c, at, by):
        value = in_ref[pair, c]
        return value if base == 0 else jnp.where(by, entry(cf_ref, 8 + at, (8 * pair + 5 if at < 4 else 8 * pair + 127) % 128), 1.0) * value

    @pl.when(upward)
    def _():
        for c in range(2):
            carry = jnp.zeros((2, 8, 128), jnp.float32)
            for pair in range(16):
                out_ref[pair, c] = carry
                carry = entry(cf_ref, base + c, 8 * pair + 1) * carry + scaled(pair, c, base + c, lower)

    @pl.when(jnp.logical_not(upward))
    def _():
        for c in range(2):
            carry = jnp.zeros((2, 8, 128), jnp.float32)
            for pair in range(15, -1, -1):
                out_ref[pair, c] = carry
                at = 4 + base + c
                kept = entry(cf_ref, at, (8 * pair + 127) % 128) * carry
                carry = kept + scaled(pair, c, at, jnp.logical_not(lower))


def crossing_kernel(own_ref, carry_ref, cf_ref, out_ref):
    for c in range(2):
        lower, r0, _, _, s1 = pair_factors(cf_ref, 2 + c)
        up, down = carry_ref[0:8, c], carry_ref[8:16, c]
        out_ref[0:8, c] = jnp.where(lower, r0 * up + own_ref[0:8, c], up)
        out_ref[8:16, c] = jnp.where(lower, down, s1 * down + own_ref[8:16, c])


def finish_kernel(
    kept, part_ref, carry01_ref, partner01_ref, carry23_ref, partner23_ref, cf_ref, out_ref
):
    core = lax.axis_index("core")
    upper = (core == 1) if kept else (core == 0)
    base = 2 * core if kept else 2 - 2 * core
    for c in range(4):
        carry_ref, partner_ref = (
            (carry01_ref, partner01_ref),
            (carry23_ref, partner23_ref),
        )[c // 2]
        lower, r0, _, _, s1 = pair_factors(cf_ref, c)
        by_p, by_q = jnp.where(lower, 1.0, r0), jnp.where(lower, s1, 1.0)
        rise, fall = weights(cf_ref, c)
        rises = [jnp.where(upper, rise[2 + k], rise[k]) for k in range(2)]
        falls = [jnp.where(upper, fall[2 + k], fall[k]) for k in range(2)]
        for half in range(2):
            here = slice(8 * half, 8 * half + 8)
            rows = pl.ds(pl.multiple_of(core * 16 + 8 * half, 8), 8) if kept else here
            for block in range(8):
                lanes = slice(128 * block, 128 * block + 128)
                up = piece(half, block, 0), c % 2, block % 2
                down = piece(half, block, 1), c % 2, block % 2
                p = by_p * carry_ref[up]
                q = by_q * carry_ref[down]
                if c < 2:
                    p = p + jnp.where(lower, 0.0, partner_ref[up])
                    q = q + jnp.where(lower, partner_ref[down], 0.0)
                else:
                    p, q = p + partner_ref[up], q + partner_ref[down]
                for k in range(2):
                    own = part_ref[c, base + k, here, lanes]
                    out_ref[c, k, rows, lanes] = own + rises[k] * p + falls[k] * q


def shards(flow_state, spacing, diffusivity):
    core = lax.axis_index("core")
    f32 = jnp.float32

    def route(value, axes, sizes, to):
        pairs = []
        for source in range(int(np.prod(sizes))):
            target = to(*(int(i) for i in np.unravel_index(source, sizes)))
            if target is not None:
                pairs.append((source, target))
        return lax.ppermute(value, axes, pairs)

    def across_cores(value):
        return lax.ppermute(value, "core", [(0, 1), (1, 0)])

    def within(chip, k):
        return 2 * chip + k if 0 <= chip < 32 else None

    def to_chip(chip, k):
        return within(chip + 1 if k else chip - 1, 1 - k)

    def to_col(k, z):
        return (1 - k) * 8 + (z + (1 if k else -1)) % 8

    other = across_cores(flow_state)
    edge = lax.dynamic_slice(flow_state, (2, core, 0, 0), (1, 1, 32, 1024)).reshape(32, 1024)
    w_far = route(edge, ROW, (32, 2), to_chip)
    ends = pl.pallas_call(
        ends_kernel,
        out_shape=jax.ShapeDtypeStruct((16, 1024), f32),
        in_specs=[whole(pltpu.HBM), whole()],
        out_specs=whole(),
        scratch_shapes=[pltpu.VMEM((4, 2, 8, 1024), f32), pltpu.SemaphoreType.DMA],
        compiler_params=params(),
        name="row_ends",
    )(flow_state, other)
    halo = route(ends, ("core", "zl"), (2, 8), to_col)

    own_cf, scan_cf = pl.pallas_call(
        coefficients_kernel,
        out_shape=(jax.ShapeDtypeStruct((24, 128), f32), jax.ShapeDtypeStruct((16, 128), f32)),
        in_specs=[whole(), whole(pltpu.SMEM)],
        out_specs=(whole(), whole()),
        compiler_params=params(),
        name="coefficients",
    )(spacing.reshape(1, 128), diffusivity)

    def call(kernel, name, outs, *args, **more):
        smem = {id(own_cf), id(diffusivity)} if kernel is local_kernel else set()
        return pl.pallas_call(
            kernel,
            out_shape=outs,
            in_specs=[whole(pltpu.SMEM if id(a) in smem else pltpu.VMEM) for a in args],
            out_specs=jax.tree.map(lambda _: whole(), outs),
            compiler_params=params(),
            name=name,
            **more,
        )(*args)

    def in_plane(value):
        return lax.all_to_all(value, ("y", "x"), split_axis=0, concat_axis=0, tiled=True)

    def to_partner(value):
        return lax.ppermute(value, "zh", [(0, 1), (1, 0)])

    def sent_back(value, base):
        kernel = functools.partial(scan_kernel, base)
        return in_plane(call(kernel, "scan_pairs", pieces, value, scan_cf))

    def in_loop(step, value):
        def body(state):
            left, held = lax.optimization_barrier((state[0] - 1, state[1]))
            return left, step(held)

        once = lax.optimization_barrier(jnp.int32(1))
        return lax.while_loop(lambda state: state[0] > 0, body, (once, value))[1]

    def array(*shape):
        return jax.ShapeDtypeStruct(shape, f32)

    pieces = array(16, 2, 2, 8, 128)
    halo, w_far, own_cf, scan_cf = lax.optimization_barrier((halo, w_far, own_cf, scan_cf))
    w_near = across_cores(w_far)
    part, raw01, raw23 = call(
        local_kernel,
        "local_step",
        (array(4, 4, 16, 1024), pieces, pieces),
        flow_state, other, halo, own_cf, diffusivity,
    )
    sum01, sum23, part = call(
        edges_kernel,
        "edge_products",
        (pieces, pieces, array(4, 4, 16, 1024)),
        flow_state, other, w_far, w_near, raw01, raw23, part, own_cf,
        input_output_aliases={4: 0, 5: 1, 6: 2},
    )

    partner01 = to_partner(sum01)
    carry23 = in_loop(lambda value: sent_back(in_plane(value), 2), sum23)
    leaving23 = call(crossing_kernel, "crossing", pieces, sum23, carry23, own_cf)
    partner23 = to_partner(leaving23)

    def scan_pairs01(value):
        moments = call(pair_kernel, "pair_moments", pieces, value, partner01, own_cf)
        return sent_back(in_plane(moments), 0)

    sum01, _ = lax.optimization_barrier((sum01, leaving23))
    carry01 = in_loop(scan_pairs01, sum01)
    ready = part, carry01, partner01, carry23, partner23, own_cf
    leaving = call(
        functools.partial(finish_kernel, False), "finish_other", array(4, 2, 16, 1024), *ready
    )
    back = across_cores(leaving)
    kept = call(functools.partial(finish_kernel, True), "finish_own", array(4, 2, 32, 1024), *ready)
    return lax.dynamic_update_slice_in_dim(kept, back, 16 * (1 - core), 2)


def solution(mesh):
    fine = Mesh(mesh.devices.reshape(4, 4, 2, 2, 8), AXES)
    field = P(None, ROW, "zl", None)
    return jax.shard_map(
        shards, mesh=fine, in_specs=(field, P(), P()), out_specs=field, check_vma=False
    )
```

```python
import functools

import jax
import jax.numpy as jnp
import numpy as np
from jax import lax
from jax.experimental import pallas as pl
from jax.experimental.pallas import tpu as pltpu
from jax.sharding import Mesh
from jax.sharding import PartitionSpec as P

time_step = 0.02
cell_width = 0.1
buoyancy = 1.0

AXES = ("y", "x", "zh", "core", "zl")
ROW = AXES[:4]
PLANE = AXES[:3]
LIMIT = 12 * 2**20


def whole(space=pltpu.VMEM):
    return pl.BlockSpec(memory_space=space)


def params():
    return pltpu.CompilerParams(vmem_limit_bytes=LIMIT)


def prefix(matrix, lane, backward):
    a, b, c, d = matrix
    step = 1
    while step < 128:
        by = 128 - step if backward else step
        edge = lane >= 128 - step if backward else lane < step
        pa, pb, pc, pd = (pltpu.roll(m, by, 1) for m in (a, b, c, d))
        pa, pb = jnp.where(edge, 1.0, pa), jnp.where(edge, 0.0, pb)
        pc, pd = jnp.where(edge, 0.0, pc), jnp.where(edge, 1.0, pd)
        a, b, c, d = a * pa + b * pc, a * pb + b * pd, c * pa + d * pc, c * pb + d * pd
        scale = 1.0 / (a + b + c + d)
        a, b, c, d = a * scale, b * scale, c * scale, d * scale
        step *= 2
    return (a + b) / (c + d)


def chip_index():
    return (lax.axis_index("y") * 4 + lax.axis_index("x")) * 2 + lax.axis_index("zh")


def coefficients_kernel(spacing_ref, diffusivity_ref, own_ref, scan_ref):
    shape = (8, 128)
    lane = lax.broadcasted_iota(jnp.int32, shape, 1)
    row = lax.broadcasted_iota(jnp.int32, shape, 0)
    below = jnp.broadcast_to(spacing_ref[...], shape)
    above = jnp.where(lane == 127, below, pltpu.roll(below, 127, 1))
    across = below + above
    rate = jnp.full(shape, diffusivity_ref[3], jnp.float32)
    for component in range(3):
        rate = jnp.where(row % 4 == component, diffusivity_ref[component], rate)
    rate = time_step * rate
    low, up = 2.0 * rate / (across * below), 2.0 * rate / (across * above)
    up_before = jnp.where(lane == 0, 0.0, pltpu.roll(up, 1, 1))
    low_after = jnp.where(lane == 127, 0.0, pltpu.roll(low, 127, 1))
    one = jnp.ones(shape, jnp.float32)
    t = prefix((1.0 + low, up_before, one, up_before), lane, False)
    tau = prefix((1.0 + up, low_after, one, low_after), lane, True)
    r = jnp.where(lane == 0, 0.0, low / (low + tau))
    s = jnp.where(lane == 127, 0.0, up / (up + t))
    g = 1.0 / (t + tau - 1.0)
    rs = jnp.where(row < 4, r, s)
    gc = jnp.where(row < 4, g, time_step / across)
    four = rs * pltpu.roll(rs, 127, 1)
    four = four * pltpu.roll(four, 126, 1)
    scan_ref[0:8, :] = four * pltpu.roll(four, 124, 1)
    scan_ref[8:16, :] = four
    turn = lax.rem(129 - 4 * chip_index(), 128)
    own_ref[0:8, :] = pltpu.roll(rs, turn, 1)
    own_ref[8:16, :] = pltpu.roll(gc, turn, 1)
    own_ref[16:24, :] = pltpu.roll(four, turn, 1)
    own_ref[24:32, :] = rate * (1.0 / cell_width**2)


def entry(ref, row, lane):
    return ref[row : row + 1, lane : lane + 1]


def pair_factors(cf_ref, c):
    lower = lax.axis_index("zh") == 0
    r0 = jnp.where(lower, entry(cf_ref, 16 + c, 2), entry(cf_ref, 16 + c, 126))
    r1 = jnp.where(lower, entry(cf_ref, 16 + c, 6), entry(cf_ref, 16 + c, 2))
    s0 = jnp.where(lower, entry(cf_ref, 20 + c, 0), entry(cf_ref, 20 + c, 124))
    s1 = jnp.where(lower, entry(cf_ref, 20 + c, 4), entry(cf_ref, 20 + c, 0))
    return lower, r0, r1, s0, s1


def piece(half, block, down):
    return 8 * down + 4 * half + block // 2


def ends_kernel(own_ref, other_ref, out_ref, held, arrived):
    core = lax.axis_index("core")
    first = core == 0
    rows = pl.ds(pl.multiple_of(24 * core, 8), 8)
    fetch = pltpu.make_async_copy(own_ref.at[:, :, rows, :], held, arrived)
    fetch.start()
    for c in range(4):
        for k in range(2):
            row = jnp.where(first, other_ref[c, k, 0:1, :], other_ref[c, k, 31:32, :])
            out_ref[8 + 2 * c + k : 9 + 2 * c + k, :] = row
    fetch.wait()
    for c in range(4):
        for k in range(2):
            row = jnp.where(first, held[c, k, 0:1, :], held[c, k, 7:8, :])
            out_ref[2 * c + k : 2 * c + k + 1, :] = row


def local_kernel(own_ref, other_ref, halo_ref, cf_ref, part_ref, *send_refs):
    core = lax.axis_index("core")
    first = core == 0
    sub = lax.broadcasted_iota(jnp.int32, (8, 1024), 0)
    rate = time_step / (2.0 * cell_width)

    def tile(c, level, rows):
        return jnp.where(
            core == level // 2, own_ref[c, level % 2, rows, :], other_ref[c, level % 2, rows, :]
        )

    def far(c, level):
        line = 2 * c + level % 2
        return jnp.where(
            core == level // 2, halo_ref[8 + line : 9 + line, :], halo_ref[line : line + 1, :]
        )

    for half in range(2):
        rows = pl.ds(pl.multiple_of(core * 16 + 8 * half, 8), 8)
        here = slice(8 * half, 8 * half + 8)
        u = [tile(0, level, rows) * rate for level in range(4)]
        v = [tile(1, level, rows) * rate for level in range(4)]
        w = [tile(2, level, rows) for level in range(4)]
        wc = [w[level] * entry(cf_ref, 12, level + 1) for level in range(4)]
        for c in range(4):
            r = [entry(cf_ref, c, j) for j in range(6)]
            s = [entry(cf_ref, 4 + c, j) for j in range(6)]
            g = [entry(cf_ref, 8 + c, j) for j in range(6)]
            spread = entry(cf_ref, 24 + c, 0)
            q = w if c == 2 else [tile(c, level, rows) for level in range(4)]
            gs = []
            for level in range(4):
                centre = q[level]
                left, right = pltpu.roll(centre, 1, 1), pltpu.roll(centre, 1023, 1)
                if half == 0:
                    top = jnp.where(first, far(c, level), tile(c, level, slice(15, 16)))
                    bottom = tile(c, level, pl.ds(pl.multiple_of(core * 16 + 8, 8), 8))[:1]
                else:
                    top = tile(c, level, pl.ds(pl.multiple_of(core * 16, 8), 8))[7:]
                    bottom = jnp.where(first, tile(c, level, slice(16, 17)), far(c, level))
                front = jnp.where(sub == 0, top, pltpu.roll(centre, 1, 0))
                back = jnp.where(sub == 7, bottom, pltpu.roll(centre, 7, 0))
                total = centre + spread * ((left + right) + (front + back) - 4.0 * centre)
                total = total - u[level] * (right - left) - v[level] * (back - front)
                if level == 0:
                    total = total - wc[0] * q[1]
                elif level == 3:
                    total = total + wc[3] * q[2]
                else:
                    total = total - wc[level] * (q[level + 1] - q[level - 1])
                if c == 2:
                    total = total + (time_step * buoyancy) * tile(3, level, rows)
                elif c == 3:
                    total = total + time_step * w[level]
                gs.append(g[level + 1] * total)
            a = [gs[0]]
            for level in range(1, 4):
                a.append(r[level + 1] * a[-1] + gs[level])
            p = r[5] * a[3]
            part_ref[c, 3, here, :] = a[3]
            b = s[3] * gs[3]
            part_ref[c, 2, here, :] = a[2] + b
            for level in (1, 0):
                b = s[level + 1] * (b + gs[level + 1])
                part_ref[c, level, here, :] = a[level] + b
            b = s[0] * (b + gs[0])
            for block in range(8):
                lanes = slice(128 * block, 128 * block + 128)
                send_refs[c // 2][piece(half, block, 0), c % 2, block % 2] = p[:, lanes]
                send_refs[c // 2][piece(half, block, 1), c % 2, block % 2] = b[:, lanes]


def weights(cf_ref, c):
    r = [entry(cf_ref, c, j) for j in range(6)]
    s = [entry(cf_ref, 4 + c, j) for j in range(6)]
    rise = [1.0, r[2], r[2] * r[3], r[2] * r[3] * r[4]]
    return rise, [s[1] * s[2] * s[3], s[2] * s[3], s[3], 1.0]


def edges_kernel(
    own_ref, other_ref, far_ref, near_ref, raw01_ref, raw23_ref, old_ref, cf_ref,
    sum01_ref, sum23_ref, part_ref,
):
    core = lax.axis_index("core")
    first = core == 0
    for half in range(2):
        rows = pl.ds(pl.multiple_of(core * 16 + 8 * half, 8), 8)
        far, near = far_ref[rows, :], near_ref[rows, :]
        w_low = jnp.where(first, far, near) * -entry(cf_ref, 12, 0)
        w_high = jnp.where(first, near, far) * entry(cf_ref, 12, 5)
        for c in range(4):
            raw_ref, sum_ref = ((raw01_ref, sum01_ref), (raw23_ref, sum23_ref))[c // 2]
            r = [entry(cf_ref, c, j) for j in range(6)]
            s = [entry(cf_ref, 4 + c, j) for j in range(6)]
            lowest = jnp.where(first, own_ref[c, 0, rows, :], other_ref[c, 0, rows, :])
            highest = jnp.where(first, other_ref[c, 1, rows, :], own_ref[c, 1, rows, :])
            low, high = entry(cf_ref, 8 + c, 0) * (w_low * lowest), entry(cf_ref, 8 + c, 5) * (w_high * highest)
            from_low, from_high = r[1] * low, s[4] * high
            p = (r[2] * r[3] * r[4] * r[5]) * from_low + high
            q = (s[0] * s[1] * s[2] * s[3]) * from_high + low
            for block in range(8):
                lanes = slice(128 * block, 128 * block + 128)
                up = piece(half, block, 0), c % 2, block % 2
                down = piece(half, block, 1), c % 2, block % 2
                sum_ref[up] = raw_ref[up] + p[:, lanes]
                sum_ref[down] = raw_ref[down] + q[:, lanes]
            rise, fall = weights(cf_ref, c)
            here = slice(8 * half, 8 * half + 8)
            for level in range(4):
                part_ref[c, level, here, :] = old_ref[c, level, here, :] + (
                    rise[level] * from_low + fall[level] * from_high
                )


def pair_kernel(own_ref, partner_ref, cf_ref, out_ref):
    for c in range(2):
        lower, _, r1, s0, _ = pair_factors(cf_ref, c)
        own_p, partner_p = jnp.where(lower, r1, 1.0), jnp.where(lower, 1.0, r1)
        own_q, partner_q = jnp.where(lower, 1.0, s0), jnp.where(lower, s0, 1.0)
        out_ref[0:8, c] = own_p * own_ref[0:8, c] + partner_p * partner_ref[0:8, c]
        out_ref[8:16, c] = own_q * own_ref[8:16, c] + partner_q * partner_ref[8:16, c]


def scan_kernel(base, in_ref, cf_ref, out_ref):
    upward = lax.axis_index("y") < 2
    lower = lax.axis_index("zh") == 0

    def scaled(pair, c, at, by):
        value = in_ref[pair, c]
        return value if base == 0 else jnp.where(by, entry(cf_ref, 8 + at, (8 * pair + 5 if at < 4 else 8 * pair + 127) % 128), 1.0) * value

    @pl.when(upward)
    def _():
        for c in range(2):
            carry = jnp.zeros((2, 8, 128), jnp.float32)
            for pair in range(16):
                out_ref[pair, c] = carry
                carry = entry(cf_ref, base + c, 8 * pair + 1) * carry + scaled(pair, c, base + c, lower)

    @pl.when(jnp.logical_not(upward))
    def _():
        for c in range(2):
            carry = jnp.zeros((2, 8, 128), jnp.float32)
            for pair in range(15, -1, -1):
                out_ref[pair, c] = carry
                at = 4 + base + c
                kept = entry(cf_ref, at, (8 * pair + 127) % 128) * carry
                carry = kept + scaled(pair, c, at, jnp.logical_not(lower))


def crossing_kernel(own_ref, carry_ref, cf_ref, out_ref):
    for c in range(2):
        lower, r0, _, _, s1 = pair_factors(cf_ref, 2 + c)
        up, down = carry_ref[0:8, c], carry_ref[8:16, c]
        out_ref[0:8, c] = jnp.where(lower, r0 * up + own_ref[0:8, c], up)
        out_ref[8:16, c] = jnp.where(lower, down, s1 * down + own_ref[8:16, c])


def finish_kernel(
    kept, part_ref, carry01_ref, partner01_ref, carry23_ref, partner23_ref, cf_ref, out_ref
):
    core = lax.axis_index("core")
    upper = (core == 1) if kept else (core == 0)
    base = 2 * core if kept else 2 - 2 * core
    for c in range(4):
        carry_ref, partner_ref = (
            (carry01_ref, partner01_ref),
            (carry23_ref, partner23_ref),
        )[c // 2]
        lower, r0, _, _, s1 = pair_factors(cf_ref, c)
        by_p, by_q = jnp.where(lower, 1.0, r0), jnp.where(lower, s1, 1.0)
        rise, fall = weights(cf_ref, c)
        rises = [jnp.where(upper, rise[2 + k], rise[k]) for k in range(2)]
        falls = [jnp.where(upper, fall[2 + k], fall[k]) for k in range(2)]
        for half in range(2):
            here = slice(8 * half, 8 * half + 8)
            rows = pl.ds(pl.multiple_of(core * 16 + 8 * half, 8), 8) if kept else here
            for block in range(8):
                lanes = slice(128 * block, 128 * block + 128)
                up = piece(half, block, 0), c % 2, block % 2
                down = piece(half, block, 1), c % 2, block % 2
                p = by_p * carry_ref[up]
                q = by_q * carry_ref[down]
                if c < 2:
                    p = p + jnp.where(lower, 0.0, partner_ref[up])
                    q = q + jnp.where(lower, partner_ref[down], 0.0)
                else:
                    p, q = p + partner_ref[up], q + partner_ref[down]
                for k in range(2):
                    own = part_ref[c, base + k, here, lanes]
                    out_ref[c, k, rows, lanes] = own + rises[k] * p + falls[k] * q


def shards(flow_state, spacing, diffusivity):
    core = lax.axis_index("core")
    f32 = jnp.float32

    def route(value, axes, sizes, to):
        pairs = []
        for source in range(int(np.prod(sizes))):
            target = to(*(int(i) for i in np.unravel_index(source, sizes)))
            if target is not None:
                pairs.append((source, target))
        return lax.ppermute(value, axes, pairs)

    def across_cores(value):
        return lax.ppermute(value, "core", [(0, 1), (1, 0)])

    def within(chip, k):
        return 2 * chip + k if 0 <= chip < 32 else None

    def to_chip(chip, k):
        return within(chip + 1 if k else chip - 1, 1 - k)

    def to_col(k, z):
        return (1 - k) * 8 + (z + (1 if k else -1)) % 8

    other = across_cores(flow_state)
    edge = lax.dynamic_slice(flow_state, (2, core, 0, 0), (1, 1, 32, 1024)).reshape(32, 1024)
    w_far = route(edge, ROW, (32, 2), to_chip)
    ends = pl.pallas_call(
        ends_kernel,
        out_shape=jax.ShapeDtypeStruct((16, 1024), f32),
        in_specs=[whole(pltpu.HBM), whole()],
        out_specs=whole(),
        scratch_shapes=[pltpu.VMEM((4, 2, 8, 1024), f32), pltpu.SemaphoreType.DMA],
        compiler_params=params(),
        name="row_ends",
    )(flow_state, other)
    halo = route(ends, ("core", "zl"), (2, 8), to_col)

    own_cf, scan_cf = pl.pallas_call(
        coefficients_kernel,
        out_shape=(jax.ShapeDtypeStruct((32, 128), f32), jax.ShapeDtypeStruct((16, 128), f32)),
        in_specs=[whole(), whole(pltpu.SMEM)],
        out_specs=(whole(), whole()),
        compiler_params=params(),
        name="coefficients",
    )(spacing.reshape(1, 128), diffusivity)

    def call(kernel, name, outs, *args, **more):
        return pl.pallas_call(
            kernel,
            out_shape=outs,
            in_specs=[whole() for _ in args],
            out_specs=jax.tree.map(lambda _: whole(), outs),
            compiler_params=params(),
            name=name,
            **more,
        )(*args)

    def in_plane(value):
        return lax.all_to_all(value, ("y", "x"), split_axis=0, concat_axis=0, tiled=True)

    def to_partner(value):
        return lax.ppermute(value, "zh", [(0, 1), (1, 0)])

    def sent_back(value, base):
        kernel = functools.partial(scan_kernel, base)
        return in_plane(call(kernel, "scan_pairs", pieces, value, scan_cf))

    def in_loop(step, value):
        def body(state):
            left, held = lax.optimization_barrier((state[0] - 1, state[1]))
            return left, step(held)

        once = lax.optimization_barrier(jnp.int32(1))
        return lax.while_loop(lambda state: state[0] > 0, body, (once, value))[1]

    def array(*shape):
        return jax.ShapeDtypeStruct(shape, f32)

    pieces = array(16, 2, 2, 8, 128)
    halo, w_far, own_cf, scan_cf = lax.optimization_barrier((halo, w_far, own_cf, scan_cf))
    w_near = across_cores(w_far)
    part, raw01, raw23 = call(
        local_kernel,
        "local_step",
        (array(4, 4, 16, 1024), pieces, pieces),
        flow_state, other, halo, own_cf,
    )
    sum01, sum23, part = call(
        edges_kernel,
        "edge_products",
        (pieces, pieces, array(4, 4, 16, 1024)),
        flow_state, other, w_far, w_near, raw01, raw23, part, own_cf,
        input_output_aliases={4: 0, 5: 1, 6: 2},
    )

    partner01 = to_partner(sum01)
    carry23 = in_loop(lambda value: sent_back(in_plane(value), 2), sum23)
    leaving23 = call(crossing_kernel, "crossing", pieces, sum23, carry23, own_cf)
    partner23 = to_partner(leaving23)

    def scan_pairs01(value):
        moments = call(pair_kernel, "pair_moments", pieces, value, partner01, own_cf)
        return sent_back(in_plane(moments), 0)

    sum01, _ = lax.optimization_barrier((sum01, leaving23))
    carry01 = in_loop(scan_pairs01, sum01)
    ready = part, carry01, partner01, carry23, partner23, own_cf
    leaving = call(
        functools.partial(finish_kernel, False), "finish_other", array(4, 2, 16, 1024), *ready
    )
    back = across_cores(leaving)
    kept = call(functools.partial(finish_kernel, True), "finish_own", array(4, 2, 32, 1024), *ready)
    return lax.dynamic_update_slice_in_dim(kept, back, 16 * (1 - core), 2)


def solution(mesh):
    fine = Mesh(mesh.devices.reshape(4, 4, 2, 2, 8), AXES)
    field = P(None, ROW, "zl", None)
    return jax.shard_map(
        shards, mesh=fine, in_specs=(field, P(), P()), out_specs=field, check_vma=False
    )
```
